256 devices in a mesh: space: 256 (over z, x, y, core).
Axes of the slice: x: 4, y: 4, z: 8, core: 2. Of those that a mesh axis runs over, the one named last changes fastest.
Arguments:
- panel: float32 [129, 4194304], P(None, 'space'), as said below
- eig_table: float32 [128, 128], replicated, may hold values from -0.5 to 0.5
- mode_index: int32 [16], replicated, may hold values from 0 to 127
- mode_coef: float32 [16], replicated, may hold values from -4 to 4
Outputs:
- modes: float32 [16, 4194304], P(None, 'space')
- operator: float32 [128, 128], replicated
- first_factor: float32 [128, 128], replicated
The draws below stay inside these ranges and needn't reach their ends.
Inputs may be any that keep to these rules, and one draw needn't show every extreme that they name: `mode_index`: each entry names a column of eig_table; entries may repeat. `panel`: Real-valued snapshots whose rows have full rank over the grid.
All inputs are finite; a program needn't handle non-finite values.
Results may differ from the reference program's by a relative error of at most 0.00035.
Values sent between devices are 32-bit elements; how exact they have to be, the bound alone decides.
No kernel may reach another device: no remote copies, remote signals or barrier semaphores. Data moves between devices by JAX's collectives and lax.ppermute only.
A program may use at most 128 MiB of HBM per device.

```python
import jax
import jax.numpy as jnp
from jax import lax

WINDOW = 128
MODES = 16
SNAPS = 129
ROWS = 4194304


def draw_panel(key, part):
    key = jax.random.fold_in(key, 1)
    key_common, key_noise, key_scale = jax.random.split(key, 3)
    common = jax.random.normal(key_common, (1, ROWS), jnp.float32)
    scales = jnp.exp(jax.random.uniform(key_scale, (SNAPS, 1), jnp.float32) * jnp.log(10.0))
    envelope = 1.0 + 3.0 * jnp.arange(ROWS, dtype=jnp.float32)[None, :] / ROWS
    noise = jax.random.normal(key_noise, (SNAPS, ROWS), jnp.float32)
    mixing = 10.0
    return scales * envelope * (mixing * common + noise)


def touch_ends(drawn, stream_key, smallest, high):
    shape = drawn.shape
    spot = [jax.random.randint(jax.random.fold_in(stream_key, axis), (), 0, shape[axis]) for axis in range(len(shape))]
    drawn = drawn.at[tuple(spot)].set(smallest)
    longest = shape.index(max(shape))
    spot[longest] = (spot[longest] + 1) % shape[longest]
    return drawn.at[tuple(spot)].set(high)


def centred(own_key, dims, scale, limit, kind=jnp.bfloat16):
    values = scale * jax.random.normal(own_key, dims, jnp.float32)
    return jnp.clip(values, min=-limit, max=limit).astype(kind)


def setup_inputs(seed: int = 0) -> dict:
    arg_keys = jax.random.split(jax.random.key(seed), 5)
    return {
        "panel": draw_panel(jax.random.fold_in(arg_keys[4], 71), 0),
        "eig_table": centred(arg_keys[1], (WINDOW, WINDOW), WINDOW ** -0.5, 0.5, jnp.float32),
        "mode_index": touch_ends(jax.random.randint(arg_keys[2], (MODES,), 0, WINDOW), jax.random.fold_in(arg_keys[2], 1), 0, WINDOW - 1).astype(jnp.int32),
        "mode_coef": centred(arg_keys[3], (MODES,), 1.0, 4.0, jnp.float32),
    }


HIGH = lax.Precision.HIGHEST

def small_factor(block):
    count = block.shape[0]
    places = jnp.arange(count, dtype=jnp.int32)
    lower = jnp.zeros_like(block)
    for column in range(count):
        prior = lower[column, :]
        diag_value = jnp.sqrt(block[column, column] - jnp.sum(prior * prior))
        fresh = (block[:, column] - jnp.dot(lower, prior, precision=HIGH)) / diag_value
        fresh = jnp.where(places >= column, fresh, jnp.zeros_like(fresh))
        lower = lower.at[:, column].set(fresh)
    identity = jnp.eye(count, dtype=block.dtype)
    inverse = jnp.zeros_like(block)
    for row in range(count):
        fresh = (identity[row] - jnp.dot(lower[row], inverse, precision=HIGH)) / lower[row, row]
        inverse = inverse.at[row].set(fresh)
    return (lower, inverse)

def lower_factor(gram):
    count = gram.shape[0]
    if count <= 16:
        return small_factor(gram)
    half = count // 2
    upper_lower, upper_inverse = lower_factor(gram[:half, :half])
    corner = jnp.dot(gram[half:, :half], upper_inverse.T, precision=HIGH)
    rest = gram[half:, half:] - jnp.dot(corner, corner.T, precision=HIGH)
    rest_lower, rest_inverse = lower_factor(rest)
    blank = jnp.zeros((half, count - half), gram.dtype)
    lower = jnp.concatenate([jnp.concatenate([upper_lower, blank], axis=1), jnp.concatenate([corner, rest_lower], axis=1)], axis=0)
    mixed = -jnp.dot(rest_inverse, jnp.dot(corner, upper_inverse, precision=HIGH), precision=HIGH)
    inverse = jnp.concatenate([jnp.concatenate([upper_inverse, blank], axis=1), jnp.concatenate([mixed, rest_inverse], axis=1)], axis=0)
    return (lower, inverse)

def inverse_upper(gram):
    lower, inverse = lower_factor(gram)
    return (lower.T, inverse.T)

def reference(panel, eig_table, mode_index, mode_coef):
    past = panel[:WINDOW]
    future = panel[1:]
    first_gram = jnp.dot(past, past.T, precision=HIGH)
    first_upper, first_inverse = inverse_upper(first_gram)
    root = jnp.sqrt(jnp.asarray(ROWS, panel.dtype))
    first_factor = first_upper / root
    basis_one = jnp.dot(first_inverse.T, past, precision=HIGH)
    second_gram = jnp.dot(basis_one, basis_one.T, precision=HIGH)
    second_upper, second_inverse = inverse_upper(second_gram)
    basis = jnp.dot(second_inverse.T, basis_one, precision=HIGH)
    whole_inverse = jnp.dot(first_inverse, second_inverse, precision=HIGH)
    projected = jnp.dot(basis, future.T, precision=HIGH)
    operator = jnp.dot(projected, whole_inverse, precision=HIGH)
    onehot = (jnp.arange(WINDOW, dtype=jnp.int32)[:, None] == mode_index[None, :]).astype(panel.dtype)
    chosen = jnp.dot(eig_table, onehot, precision=HIGH)
    factor = mode_coef * root
    combined = jnp.dot(whole_inverse, chosen, precision=HIGH) * factor[None, :]
    modes = jnp.dot(combined.T, future, precision=HIGH)
    return (modes, operator, first_factor)
```

```python
import functools

import jax
import jax.numpy as jnp
from jax import lax
from jax.experimental import pallas as pl
from jax.experimental.pallas import tpu as pltpu
from jax.sharding import PartitionSpec as P

HIGH = lax.Precision.HIGHEST
F32 = jnp.float32
BF16 = jnp.bfloat16
NT = (((1,), (1,)), ((), ()))
NN = (((1,), (0,)), ((), ()))
TN = (((0,), (0,)), ((), ()))
PACK = 72


def dot(a, b, dims, precision=None):
    return lax.dot_general(a, b, dims, precision=precision, preferred_element_type=F32)


def two_sum(a, b):
    total = a + b
    other = total - a
    return total, (a - (total - other)) + (b - other)


def split3(x):
    high = x.astype(BF16)
    rest = x - high.astype(F32)
    mid = rest.astype(BF16)
    return high, mid, (rest - mid.astype(F32)).astype(BF16)


def iota(shape, axis):
    return lax.broadcasted_iota(jnp.int32, shape, axis)


def gram_body(steps, part, x_ref, out_ref, high_ref, low_ref, cross_ref, mid_ref, last_ref):
    step = pl.program_id(0)

    @pl.when(step == 0)
    def _():
        for ref in (high_ref, low_ref, cross_ref, mid_ref, last_ref):
            ref[...] = jnp.zeros_like(ref)

    for start in range(0, x_ref.shape[1], part):
        x = x_ref[0:128, start : start + part]
        high, mid, low = split3(x)
        both = jnp.concatenate([high, mid], axis=0)
        main = dot(both, both, NT)
        side = dot(both, low, NT)
        total, rest = two_sum(high_ref[...], main[:128, :128])
        high_ref[...] = total
        low_ref[...] += rest
        cross_ref[...] += main[:128, 128:] + (side[:128] + side[128:])
        mid_ref[...] += main[128:, 128:]
        end = x_ref[128:129, start : start + part]
        partial = x[:, 0:128] * end[:, 0:128]
        for tile in range(128, part, 128):
            partial = partial + x[:, tile : tile + 128] * end[:, tile : tile + 128]
        last_ref[...] += partial

    @pl.when(step == steps - 1)
    def _():
        cross = cross_ref[...]
        rest = low_ref[...] + (mid_ref[...] + (cross + cross.T))
        high, low = two_sum(high_ref[...], rest)
        turned = last_ref[...].T
        end_high = turned[0:8]
        end_low = jnp.zeros_like(end_high)
        for row in range(8, 128, 8):
            end_high, error = two_sum(end_high, turned[row : row + 8])
            end_low = end_low + error
        row_high, row_low = end_high[0:1], end_low[0:1]
        for row in range(1, 8):
            row_high, error = two_sum(row_high, end_high[row : row + 1])
            row_low = row_low + (error + end_low[row : row + 1])
        out_ref[0] = pack(high, row_high)
        out_ref[1] = pack(low, row_low)


def pack(gram, last):
    rows, lanes = iota((64, 128), 0), iota((64, 128), 1)
    turned = pltpu.roll(gram[64:128], 64, 1)
    folded = jnp.where(lanes > rows, gram[0:64], jnp.where(lanes < rows, turned, 0.0))
    on_diagonal = iota((128, 128), 0) == iota((128, 128), 1)
    diagonal = jnp.sum(jnp.where(on_diagonal, gram, 0.0), axis=0, keepdims=True)
    return jnp.concatenate([folded, diagonal, last, jnp.zeros((6, 128), F32)], axis=0)


def unpack(packed):
    rows, lanes = iota((64, 128), 0), iota((64, 128), 1)
    folded = packed[0:64]
    top = jnp.where(lanes > rows, folded, 0.0)
    turned = pltpu.roll(folded, 64, 1)
    bottom = jnp.where((lanes >= 64) & (lanes - 64 < rows), turned, 0.0)
    half = jnp.concatenate([top, bottom], axis=0)
    on_diagonal = iota((128, 128), 0) == iota((128, 128), 1)
    gram = jnp.where(on_diagonal, packed[64:65], half + half.T)
    return gram, packed[65:66]


def local_gram(panel, chunk=2048, part=1024):
    snaps, columns = panel.shape
    chunk = min(chunk, columns)
    steps = columns // chunk
    square = pltpu.VMEM((128, 128), F32)
    return pl.pallas_call(
        functools.partial(gram_body, steps, min(part, chunk)),
        grid=(steps,),
        in_specs=[pl.BlockSpec((snaps, chunk), lambda i: (0, i))],
        out_specs=pl.BlockSpec((2, PACK, 128), lambda i: (0, 0, 0)),
        out_shape=jax.ShapeDtypeStruct((2, PACK, 128), F32),
        scratch_shapes=[square] * 5,
        compiler_params=pltpu.CompilerParams(vmem_limit_bytes=40 * 1024 * 1024),
        name="gram",
    )(panel)


def pair_add(a, b):
    total, rest = two_sum(a[0], b[0])
    return jnp.stack([total, (a[1] + b[1]) + rest])


def exchange(x, step, size):
    return lax.ppermute(x, "space", [(i, i ^ step) for i in range(size)])


def sum_pairs(x, size):
    step = 1
    while step < size:
        if step > 1 and step * 4 <= size:
            first = exchange(x, step, size)
            second = exchange(x, 2 * step, size)
            third = exchange(x, 3 * step, size)
            x = pair_add(pair_add(x, first), pair_add(second, third))
            step *= 4
        else:
            x = pair_add(x, exchange(x, step, size))
            step *= 2
    return x


def power_scale(square):
    scale = jnp.ones_like(square)
    inverse = jnp.ones_like(square)
    for k in (32, 16, 8, 4, 2, 1):
        big = square >= 4.0**k
        square = jnp.where(big, square * 4.0**-k, square)
        scale = jnp.where(big, scale * 2.0**-k, scale)
        inverse = jnp.where(big, inverse * 2.0**k, inverse)
    for k in (32, 16, 8, 4, 2, 1):
        small = square < 4.0 ** (1 - k)
        square = jnp.where(small, square * 4.0**k, square)
        scale = jnp.where(small, scale * 2.0**k, scale)
        inverse = jnp.where(small, inverse * 2.0**-k, inverse)
    return scale, inverse


def slices(high, low, unit, count):
    out = []
    rest = high
    for index in range(count):
        if index == 2 and low is not None:
            rest = rest + low
        magic = 1.5 * 2.0**23 * unit * 2.0 ** (-9 * index)
        piece = (rest + magic) - magic
        rest = rest - piece
        out.append(piece)
    return out


def add_levels(levels):
    total, rest = two_sum(levels[0], levels[1])
    for level in levels[2:4]:
        total, error = two_sum(total, level)
        rest = rest + error
    for level in levels[4:]:
        rest = rest + level
    return two_sum(total, rest)


def factor(matrix):
    count = 16
    work = [matrix[8 * i : 8 * i + 8] for i in range(count)]
    lanes, rows = iota((8, 128), 1), iota((8, 128), 0)
    extra = [jnp.where(lanes == rows + 8 * i, 1.0, 0.0).astype(F32) for i in range(count)]
    upper, inverse = [], []
    for block in range(count):
        at = 8 * block
        wide, carried = work[block], extra[block]
        columns = [jnp.broadcast_to(wide[:, at + k : at + k + 1], (8, 128)) for k in range(8)]
        pivots = jnp.ones((8, 128), F32)
        for j in range(8):
            pivot = jnp.broadcast_to(columns[j][j : j + 1], (8, 128))
            pivots = jnp.where(rows == j, pivot, pivots)
            if j == 7:
                break
            ratio = jnp.where(rows > j, columns[j] * (1.0 / pivot), 0.0)
            for k in range(j + 1, 8):
                columns[k] = columns[k] - ratio * jnp.broadcast_to(columns[k][j : j + 1], (8, 128))
            wide = wide - ratio * jnp.broadcast_to(wide[j : j + 1], (8, 128))
            carried = carried - ratio * jnp.broadcast_to(carried[j : j + 1], (8, 128))
        root = lax.rsqrt(pivots)
        root = root * (1.5 - 0.5 * pivots * root * root)
        wide = jnp.where(lanes >= rows + at, wide * root, 0.0)
        carried = carried * root
        upper.append(wide)
        inverse.append(carried)
        if block < count - 1:
            both = jnp.concatenate([wide, carried], axis=1)
            left = [part.astype(F32) for part in split3(wide)]
            right = [part.astype(F32) for part in split3(both)]
            order = ((0, 0), (0, 1), (1, 0), (1, 1), (0, 2), (2, 0))
            stack_left = jnp.concatenate([left[i] for i, _ in order], axis=0).T.astype(BF16)
            stack_right = jnp.concatenate([right[j] for _, j in order], axis=0).astype(BF16)
            update = dot(stack_left, stack_right, NN)
            for later in range(block + 1, count):
                work[later] = work[later] - update[8 * later : 8 * later + 8, :128]
                extra[later] = extra[later] - update[8 * later : 8 * later + 8, 128:]
    return jnp.concatenate(upper, axis=0), jnp.concatenate(inverse, axis=0)


def algebra_body(root, packed_ref, table_ref, index_ref, coef_ref, operator_ref, factor_ref, comb_ref, shift_ref):
    gram_high, last_high = unpack(packed_ref[0])
    gram_low, last_low = unpack(packed_ref[1])
    gram_high, gram_low = two_sum(gram_high, gram_low)
    last_high, last_low = two_sum(last_high, last_low)
    on_diagonal = iota((128, 128), 0) == iota((128, 128), 1)
    diagonal = jnp.sum(jnp.where(on_diagonal, gram_high, 0.0), axis=0, keepdims=True)
    scale, unscale = power_scale(diagonal)
    scale_wide = jnp.broadcast_to(scale, (128, 128))
    scale_tall = scale_wide.T
    gram_high = gram_high * scale_wide * scale_tall
    gram_low = gram_low * scale_wide * scale_tall
    last_high = last_high * scale
    last_low = last_low * scale
    biggest = jnp.max(jnp.abs(last_high), axis=1, keepdims=True)
    last_scale, last_unscale = power_scale(jnp.broadcast_to(biggest * biggest, (1, 128)))
    last_high = last_high * last_scale
    last_low = last_low * last_scale

    upper, lower_inverse = factor(gram_high)
    factor_ref[...] = upper * (unscale * (1.0 / root))

    norms = jnp.sum(lower_inverse * lower_inverse, axis=1, keepdims=True)
    row_scale, _ = power_scale(jnp.broadcast_to(norms, (128, 128)))
    y_one, y_two = slices(lower_inverse * row_scale, None, 2.0**-7, 2)
    first = y_one + y_two
    y_both = jnp.concatenate([y_one, y_two], axis=0).astype(BF16)

    blank = jnp.zeros((7, 128), F32)
    whole_high = jnp.concatenate([gram_high, last_high, blank], axis=0)
    whole_low = jnp.concatenate([gram_low, last_low, blank], axis=0)
    g = [piece.astype(BF16) for piece in slices(whole_high, whole_low, 2.0**-6, 4)]
    p = [dot(piece, y_both, NT) for piece in g]
    one = [piece[:, :128] for piece in p]
    two = [piece[:, 128:] for piece in p]
    t_high, t_low = add_levels(
        [one[0], one[1] + two[0], one[2] + two[1], one[3] + two[2], two[3]]
    )

    norms = jnp.sum(t_high[:128] * t_high[:128], axis=0, keepdims=True)
    column_scale, column_unscale = power_scale(norms)
    t = slices(t_high[:128] * column_scale, t_low[:128] * column_scale, 2.0**-7, 4)
    t_all = jnp.concatenate([piece.astype(BF16) for piece in t], axis=1)
    s = dot(y_both, t_all, NN)
    one = [s[:128, 128 * k : 128 * k + 128] for k in range(4)]
    two = [s[128:, 128 * k : 128 * k + 128] for k in range(4)]
    s_high, s_low = add_levels(
        [one[0], one[1] + two[0], one[2] + two[1], one[3] + two[2], two[3]]
    )
    _, second = factor((s_high + s_low) * column_unscale)

    whole = dot(second, first, NN, HIGH)
    shift_ref[...] = t_high
    z = shift_ref[1:129]
    following = jnp.where(iota((1, 128), 1) == 127, last_unscale, pltpu.roll(unscale, 127, 1))
    h = dot(whole * (scale * following), z, NN, HIGH)
    operator_ref[...] = dot(second, h, NT, HIGH)

    onehot = (iota((16, 128), 1) == index_ref[...]).astype(F32)
    chosen = dot(onehot, table_ref[...], NT, HIGH)
    comb_ref[...] = dot(chosen, whole, NN, HIGH) * scale * (coef_ref[...] * root)


def algebra(packed, table, index, coef, total_rows):
    root = float(total_rows) ** 0.5
    modes = index.shape[0]
    return pl.pallas_call(
        functools.partial(algebra_body, root),
        out_shape=[
            jax.ShapeDtypeStruct((128, 128), F32),
            jax.ShapeDtypeStruct((128, 128), F32),
            jax.ShapeDtypeStruct((modes, 128), F32),
        ],
        scratch_shapes=[pltpu.VMEM((136, 128), F32)],
        compiler_params=pltpu.CompilerParams(vmem_limit_bytes=40 * 1024 * 1024),
        name="algebra",
    )(packed, table, index.reshape(modes, 1), coef.reshape(modes, 1))


def modes_body(comb_ref, x_ref, out_ref):
    comb = comb_ref[...]
    shifted = jnp.where(iota(comb.shape, 1) == 0, 0.0, pltpu.roll(comb, 1, 1))
    c = split3(shifted)
    x_high, x_mid, x_low = split3(x_ref[0:128])
    left = jnp.concatenate(
        [
            jnp.concatenate([c[0], c[1]], axis=1),
            jnp.concatenate([c[1], c[0]], axis=1),
            jnp.concatenate([c[2], jnp.zeros_like(c[2])], axis=1),
        ],
        axis=0,
    )
    main = dot(left, jnp.concatenate([x_high, x_mid], axis=0), NN)
    side = dot(c[0], x_low, NN)
    tail = comb[:, 127:128] * x_ref[128:129]
    out_ref[...] = (main[0:16] + tail) + (main[16:32] + (main[32:48] + side))


def modes_of(comb, panel, chunk=2048):
    snaps, columns = panel.shape
    chunk = min(chunk, columns)
    return pl.pallas_call(
        modes_body,
        grid=(columns // chunk,),
        in_specs=[
            pl.BlockSpec(comb.shape, lambda i: (0, 0)),
            pl.BlockSpec((snaps, chunk), lambda i: (0, i)),
        ],
        out_specs=pl.BlockSpec((comb.shape[0], chunk), lambda i: (0, i)),
        out_shape=jax.ShapeDtypeStruct((comb.shape[0], columns), F32),
        compiler_params=pltpu.CompilerParams(vmem_limit_bytes=40 * 1024 * 1024),
        name="modes",
    )(comb, panel)


def local(size, panel, eig_table, mode_index, mode_coef):
    packed = sum_pairs(local_gram(panel), size)
    operator, first_factor, comb = algebra(
        packed, eig_table, mode_index, mode_coef, panel.shape[1] * size
    )
    return modes_of(comb, panel), operator, first_factor


def solution(mesh):
    return jax.shard_map(
        functools.partial(local, mesh.shape["space"]),
        mesh=mesh,
        in_specs=(P(None, "space"), P(), P(), P()),
        out_specs=(P(None, "space"), P(), P()),
        check_vma=False,
    )
```

```python
import functools

import jax
import jax.numpy as jnp
from jax import lax
from jax.experimental import pallas as pl
from jax.experimental.pallas import tpu as pltpu
from jax.sharding import PartitionSpec as P

HIGH = lax.Precision.HIGHEST
F32 = jnp.float32
BF16 = jnp.bfloat16
NT = (((1,), (1,)), ((), ()))
NN = (((1,), (0,)), ((), ()))
TN = (((0,), (0,)), ((), ()))
HALF = 40
LIMIT = 60 * 1024 * 1024


def dot(a, b, dims, precision=None):
    return lax.dot_general(a, b, dims, precision=precision, preferred_element_type=F32)


def two_sum(a, b):
    total = a + b
    other = total - a
    return total, (a - (total - other)) + (b - other)


def split3(x):
    high = x.astype(BF16)
    rest = x - high.astype(F32)
    mid = rest.astype(BF16)
    return high, mid, (rest - mid.astype(F32)).astype(BF16)


def iota(shape, axis):
    return lax.broadcasted_iota(jnp.int32, shape, axis)


def gram_body(chunk, part, panel_ref, out_ref, x_ref, high_ref, low_ref, cross_ref, mid_ref, last_ref, sems):
    count = panel_ref.shape[1] // chunk
    for index in range(count):
        fetch(panel_ref, x_ref, sems, chunk, index).start()
    for ref in (high_ref, low_ref, cross_ref, mid_ref, last_ref):
        ref[...] = jnp.zeros_like(ref)

    def step(index, carry):
        fetch(panel_ref, x_ref, sems, chunk, index).wait()
        for start in range(0, chunk, part):
            at = pl.ds(pl.multiple_of(index * chunk + start, part), part)
            x = x_ref[0:128, at]
            high, mid, low = split3(x)
            main = dot(jnp.concatenate([high, low], axis=0), jnp.concatenate([high, mid], axis=0), NT)
            total, rest = two_sum(high_ref[...], main[:128, :128])
            high_ref[...] = total
            low_ref[...] += rest
            cross_ref[...] += main[:128, 128:] + (main[128:, :128] + main[128:, 128:])
            mid_ref[...] += dot(mid, mid, NT)
            end = x_ref[128:129, at]
            partial = x[:, 0:128] * end[:, 0:128]
            for tile in range(128, part, 128):
                partial = partial + x[:, tile : tile + 128] * end[:, tile : tile + 128]
            last_ref[...] += partial
        return carry

    lax.fori_loop(0, count, step, 0)
    cross = cross_ref[...]
    rest = low_ref[...] + (mid_ref[...] + (cross + cross.T))
    high, low = two_sum(high_ref[...], rest)
    turned = last_ref[...].T
    end_high = turned[0:8]
    end_low = jnp.zeros_like(end_high)
    for row in range(8, 128, 8):
        end_high, error = two_sum(end_high, turned[row : row + 8])
        end_low = end_low + error
    row_high, row_low = end_high[0:1], end_low[0:1]
    for row in range(1, 8):
        row_high, error = two_sum(row_high, end_high[row : row + 1])
        row_low = row_low + (error + end_low[row : row + 1])
    for part_index, (gram, last) in enumerate(((high, row_high), (low, row_low))):
        packed = pack(gram, last)
        out_ref[0, part_index] = packed[:HALF]
        out_ref[1, part_index] = packed[HALF:]


def fetch(panel_ref, x_ref, sems, chunk, index):
    at = pl.ds(pl.multiple_of(index * chunk, chunk), chunk)
    return pltpu.make_async_copy(panel_ref.at[:, at], x_ref.at[:, at], sems.at[index])


def pack(gram, last):
    rows, lanes = iota((64, 128), 0), iota((64, 128), 1)
    turned = pltpu.roll(gram[64:128], 64, 1)
    folded = jnp.where(lanes > rows, gram[0:64], jnp.where(lanes < rows, turned, 0.0))
    on_diagonal = iota((128, 128), 0) == iota((128, 128), 1)
    diagonal = jnp.sum(jnp.where(on_diagonal, gram, 0.0), axis=0, keepdims=True)
    return jnp.concatenate([folded, diagonal, last, jnp.zeros((2 * HALF - 66, 128), F32)], axis=0)


def unpack(packed):
    rows, lanes = iota((64, 128), 0), iota((64, 128), 1)
    folded = packed[0:64]
    top = jnp.where(lanes > rows, folded, 0.0)
    turned = pltpu.roll(folded, 64, 1)
    bottom = jnp.where((lanes >= 64) & (lanes - 64 < rows), turned, 0.0)
    half = jnp.concatenate([top, bottom], axis=0)
    on_diagonal = iota((128, 128), 0) == iota((128, 128), 1)
    gram = jnp.where(on_diagonal, packed[64:65], half + half.T)
    return gram, packed[65:66]


def local_gram(panel, chunk=4096, part=1024):
    snaps, columns = panel.shape
    square = pltpu.VMEM((128, 128), F32)
    return pl.pallas_call(
        functools.partial(gram_body, chunk, part),
        in_specs=[pl.BlockSpec(memory_space=pl.ANY)],
        out_shape=jax.ShapeDtypeStruct((2, 2, HALF, 128), F32),
        scratch_shapes=[pltpu.VMEM((snaps, columns), F32)]
        + [square] * 5
        + [pltpu.SemaphoreType.DMA((columns // chunk,))],
        compiler_params=pltpu.CompilerParams(vmem_limit_bytes=LIMIT),
        name="gram",
    )(panel)


def pair_add(a, b):
    total, rest = two_sum(a[0], b[0])
    return jnp.stack([total, (a[1] + b[1]) + rest])


def exchange(x, pairs):
    return lax.ppermute(x, "space", pairs)


def flips(size, step):
    return [(i, i ^ step) for i in range(size)]


def sum_pairs(x, size):
    even = lax.axis_index("space") % 2 == 0
    kept = jnp.where(even, x[0], x[1])
    sent = jnp.where(even, x[1], x[0])
    half = pair_add(kept, exchange(sent, flips(size, 1)))
    for step in (2, 8):
        first = exchange(half, flips(size, step))
        second = exchange(half, flips(size, 2 * step))
        third = exchange(half, flips(size, 3 * step))
        half = pair_add(pair_add(half, first), pair_add(second, third))
    half = pair_add(half, exchange(half, flips(size, 32)))
    before = exchange(half, [(i, (i + 64) % size) for i in range(size)])
    after = exchange(half, [(i, (i - 64) % size) for i in range(size)])
    across = exchange(half, flips(size, 160))
    half = pair_add(pair_add(half, across), pair_add(before, after))
    other = exchange(half, flips(size, 1))
    return jnp.where(even, jnp.stack([half, other]), jnp.stack([other, half]))


def power_scale(square):
    scale = jnp.ones_like(square)
    inverse = jnp.ones_like(square)
    for k in (32, 16, 8, 4, 2, 1):
        big = square >= 4.0**k
        square = jnp.where(big, square * 4.0**-k, square)
        scale = jnp.where(big, scale * 2.0**-k, scale)
        inverse = jnp.where(big, inverse * 2.0**k, inverse)
    for k in (32, 16, 8, 4, 2, 1):
        small = square < 4.0 ** (1 - k)
        square = jnp.where(small, square * 4.0**k, square)
        scale = jnp.where(small, scale * 2.0**k, scale)
        inverse = jnp.where(small, inverse * 2.0**-k, inverse)
    return scale, inverse


def slices(high, low, unit, count):
    out = []
    rest = high
    for index in range(count):
        if index == 2 and low is not None:
            rest = rest + low
        magic = 1.5 * 2.0**23 * unit * 2.0 ** (-9 * index)
        piece = (rest + magic) - magic
        rest = rest - piece
        out.append(piece)
    return out


def add_levels(levels):
    total, rest = two_sum(levels[0], levels[1])
    for level in levels[2:4]:
        total, error = two_sum(total, level)
        rest = rest + error
    for level in levels[4:]:
        rest = rest + level
    return two_sum(total, rest)


def factor(matrix):
    count = 16
    work = [matrix[8 * i : 8 * i + 8] for i in range(count)]
    lanes, rows = iota((8, 128), 1), iota((8, 128), 0)
    extra = [jnp.where(lanes == rows + 8 * i, 1.0, 0.0).astype(F32) for i in range(count)]
    upper, inverse = [], []
    for block in range(count):
        at = 8 * block
        wide, carried = work[block], extra[block]
        columns = [jnp.broadcast_to(wide[:, at + k : at + k + 1], (8, 128)) for k in range(8)]
        pivots = jnp.ones((8, 128), F32)
        for j in range(8):
            pivot = jnp.broadcast_to(columns[j][j : j + 1], (8, 128))
            pivots = jnp.where(rows == j, pivot, pivots)
            if j == 7:
                break
            ratio = jnp.where(rows > j, columns[j] * (1.0 / pivot), 0.0)
            for k in range(j + 1, 8):
                columns[k] = columns[k] - ratio * jnp.broadcast_to(columns[k][j : j + 1], (8, 128))
            wide = wide - ratio * jnp.broadcast_to(wide[j : j + 1], (8, 128))
            carried = carried - ratio * jnp.broadcast_to(carried[j : j + 1], (8, 128))
        root = lax.rsqrt(pivots)
        root = root * (1.5 - 0.5 * pivots * root * root)
        wide = jnp.where(lanes >= rows + at, wide * root, 0.0)
        carried = carried * root
        upper.append(wide)
        inverse.append(carried)
        if block < count - 1:
            both = jnp.concatenate([wide, carried], axis=1)
            left = [part.astype(F32) for part in split3(wide)]
            right = [part.astype(F32) for part in split3(both)]
            order = ((0, 0), (0, 1), (1, 0), (1, 1), (0, 2), (2, 0))
            stack_left = jnp.concatenate([left[i] for i, _ in order], axis=0).T.astype(BF16)
            stack_right = jnp.concatenate([right[j] for _, j in order], axis=0).astype(BF16)
            update = dot(stack_left, stack_right, NN)
            for later in range(block + 1, count):
                work[later] = work[later] - update[8 * later : 8 * later + 8, :128]
                extra[later] = extra[later] - update[8 * later : 8 * later + 8, 128:]
    return jnp.concatenate(upper, axis=0), jnp.concatenate(inverse, axis=0)


def finish_body(
    root,
    chunk,
    out_chunk,
    packed_ref,
    table_ref,
    index_ref,
    coef_ref,
    panel_ref,
    modes_ref,
    operator_ref,
    factor_ref,
    x_ref,
    y_ref,
    shift_ref,
    in_sems,
    out_sems,
):
    columns = panel_ref.shape[1]
    for index in range(columns // chunk):
        fetch(panel_ref, x_ref, in_sems, chunk, index).start()
    gram_high, last_high = unpack(jnp.concatenate([packed_ref[0, 0], packed_ref[1, 0]], axis=0))
    gram_low, last_low = unpack(jnp.concatenate([packed_ref[0, 1], packed_ref[1, 1]], axis=0))
    gram_high, gram_low = two_sum(gram_high, gram_low)
    last_high, last_low = two_sum(last_high, last_low)
    on_diagonal = iota((128, 128), 0) == iota((128, 128), 1)
    diagonal = jnp.sum(jnp.where(on_diagonal, gram_high, 0.0), axis=0, keepdims=True)
    scale, unscale = power_scale(diagonal)
    scale_wide = jnp.broadcast_to(scale, (128, 128))
    scale_tall = scale_wide.T
    gram_high = gram_high * scale_wide * scale_tall
    gram_low = gram_low * scale_wide * scale_tall
    last_high = last_high * scale
    last_low = last_low * scale
    biggest = jnp.max(jnp.abs(last_high), axis=1, keepdims=True)
    last_scale, last_unscale = power_scale(jnp.broadcast_to(biggest * biggest, (1, 128)))
    last_high = last_high * last_scale
    last_low = last_low * last_scale

    upper, lower_inverse = factor(gram_high)
    factor_ref[...] = upper * (unscale * (1.0 / root))

    norms = jnp.sum(lower_inverse * lower_inverse, axis=1, keepdims=True)
    row_scale, _ = power_scale(jnp.broadcast_to(norms, (128, 128)))
    y_one, y_two = slices(lower_inverse * row_scale, None, 2.0**-7, 2)
    first = y_one + y_two
    y_both = jnp.concatenate([y_one, y_two], axis=0).astype(BF16)

    blank = jnp.zeros((7, 128), F32)
    whole_high = jnp.concatenate([gram_high, last_high, blank], axis=0)
    whole_low = jnp.concatenate([gram_low, last_low, blank], axis=0)
    g = [piece.astype(BF16) for piece in slices(whole_high, whole_low, 2.0**-6, 4)]
    p = [dot(piece, y_both, NT) for piece in g]
    one = [piece[:, :128] for piece in p]
    two = [piece[:, 128:] for piece in p]
    t_high, t_low = add_levels(
        [one[0], one[1] + two[0], one[2] + two[1], one[3] + two[2], two[3]]
    )

    norms = jnp.sum(t_high[:128] * t_high[:128], axis=0, keepdims=True)
    column_scale, column_unscale = power_scale(norms)
    t = slices(t_high[:128] * column_scale, t_low[:128] * column_scale, 2.0**-7, 4)
    t_all = jnp.concatenate([piece.astype(BF16) for piece in t], axis=1)
    s = dot(y_both, t_all, NN)
    one = [s[:128, 128 * k : 128 * k + 128] for k in range(4)]
    two = [s[128:, 128 * k : 128 * k + 128] for k in range(4)]
    s_high, s_low = add_levels(
        [one[0], one[1] + two[0], one[2] + two[1], one[3] + two[2], two[3]]
    )
    _, second = factor((s_high + s_low) * column_unscale)

    whole = dot(second, first, NN, HIGH)
    shift_ref[...] = t_high
    z = shift_ref[1:129]
    following = jnp.where(iota((1, 128), 1) == 127, last_unscale, pltpu.roll(unscale, 127, 1))
    h = dot(whole * (scale * following), z, NN, HIGH)
    operator_ref[...] = dot(second, h, NT, HIGH)

    onehot = (iota((16, 128), 1) == index_ref[...]).astype(F32)
    chosen = dot(onehot, table_ref[...], NT, HIGH)
    comb = dot(chosen, whole, NN, HIGH) * scale * (coef_ref[...] * root)

    for index in range(columns // chunk):
        fetch(panel_ref, x_ref, in_sems, chunk, index).wait()
    shifted = jnp.where(iota(comb.shape, 1) == 0, 0.0, pltpu.roll(comb, 1, 1))
    c = split3(shifted)
    left = jnp.concatenate(
        [
            jnp.concatenate([c[0], c[1]], axis=1),
            jnp.concatenate([c[1], c[0]], axis=1),
            jnp.concatenate([c[2], jnp.zeros_like(c[2])], axis=1),
        ],
        axis=0,
    )

    def send(index):
        at = pl.ds(pl.multiple_of(index * out_chunk, out_chunk), out_chunk)
        return pltpu.make_async_copy(y_ref.at[:, at], modes_ref.at[:, at], out_sems.at[index])

    def step(index, carry):
        at = pl.ds(pl.multiple_of(index * out_chunk, out_chunk), out_chunk)
        x_high, x_mid, x_low = split3(x_ref[0:128, at])
        main = dot(left, jnp.concatenate([x_high, x_mid], axis=0), NN)
        side = dot(c[0], x_low, NN)
        end = comb[:, 127:128] * x_ref[128:129, at]
        y_ref[:, at] = (main[0:16] + end) + (main[16:32] + (main[32:48] + side))
        send(index).start()
        return carry

    lax.fori_loop(0, columns // out_chunk, step, 0)
    for index in range(columns // out_chunk):
        send(index).wait()


def finish(packed, table, index, coef, panel, total_rows, chunk=4096, out_chunk=2048):
    root = float(total_rows) ** 0.5
    modes = index.shape[0]
    snaps, columns = panel.shape
    whole = pl.BlockSpec(memory_space=pltpu.VMEM)
    remote = pl.BlockSpec(memory_space=pl.ANY)
    return pl.pallas_call(
        functools.partial(finish_body, root, chunk, out_chunk),
        in_specs=[whole] * 4 + [remote],
        out_specs=[remote, whole, whole],
        out_shape=[
            jax.ShapeDtypeStruct((modes, columns), F32),
            jax.ShapeDtypeStruct((128, 128), F32),
            jax.ShapeDtypeStruct((128, 128), F32),
        ],
        scratch_shapes=[
            pltpu.VMEM((snaps, columns), F32),
            pltpu.VMEM((modes, columns), F32),
            pltpu.VMEM((136, 128), F32),
            pltpu.SemaphoreType.DMA((columns // chunk,)),
            pltpu.SemaphoreType.DMA((columns // out_chunk,)),
        ],
        compiler_params=pltpu.CompilerParams(vmem_limit_bytes=LIMIT),
        name="finish",
    )(packed, table, index.reshape(modes, 1), coef.reshape(modes, 1), panel)


def local(size, panel, eig_table, mode_index, mode_coef):
    packed = sum_pairs(local_gram(panel), size)
    return tuple(finish(packed, eig_table, mode_index, mode_coef, panel, panel.shape[1] * size))


def solution(mesh):
    return jax.shard_map(
        functools.partial(local, mesh.shape["space"]),
        mesh=mesh,
        in_specs=(P(None, "space"), P(), P(), P()),
        out_specs=(P(None, "space"), P(), P()),
        check_vma=False,
    )
```

```python
import functools

import jax
import jax.numpy as jnp
from jax import lax
from jax.experimental import pallas as pl
from jax.experimental.pallas import tpu as pltpu
from jax.sharding import PartitionSpec as P

HIGH = lax.Precision.HIGHEST
F32 = jnp.float32
BF16 = jnp.bfloat16
NT = (((1,), (1,)), ((), ()))
NN = (((1,), (0,)), ((), ()))
TN = (((0,), (0,)), ((), ()))
HALF = 40
LIMIT = 60 * 1024 * 1024


def dot(a, b, dims, precision=None):
    return lax.dot_general(a, b, dims, precision=precision, preferred_element_type=F32)


def two_sum(a, b):
    total = a + b
    other = total - a
    return total, (a - (total - other)) + (b - other)


def split3(x):
    high = x.astype(BF16)
    rest = x - high.astype(F32)
    mid = rest.astype(BF16)
    return high, mid, (rest - mid.astype(F32)).astype(BF16)


def iota(shape, axis):
    return lax.broadcasted_iota(jnp.int32, shape, axis)


def gram_body(chunk, part, panel_ref, kept_ref, sent_ref, x_ref, high_ref, low_ref, cross_ref, mid_ref, last_ref, sems):
    count = panel_ref.shape[1] // chunk
    for index in range(count):
        fetch(panel_ref, x_ref, sems, chunk, index).start()
    for ref in (high_ref, low_ref, cross_ref, mid_ref, last_ref):
        ref[...] = jnp.zeros_like(ref)

    def step(index, carry):
        fetch(panel_ref, x_ref, sems, chunk, index).wait()
        for start in range(0, chunk, part):
            at = pl.ds(pl.multiple_of(index * chunk + start, part), part)
            x = x_ref[0:128, at]
            high, mid, low = split3(x)
            main = dot(jnp.concatenate([high, low], axis=0), jnp.concatenate([high, mid], axis=0), NT)
            total, rest = two_sum(high_ref[...], main[:128, :128])
            high_ref[...] = total
            low_ref[...] += rest
            cross_ref[...] += main[:128, 128:] + (main[128:, :128] + main[128:, 128:])
            mid_ref[...] += dot(mid, mid, NT)
            end = x_ref[128:129, at]
            partial = x[:, 0:128] * end[:, 0:128]
            for tile in range(128, part, 128):
                partial = partial + x[:, tile : tile + 128] * end[:, tile : tile + 128]
            last_ref[...] += partial
        return carry

    lax.fori_loop(0, count, step, 0)
    cross = cross_ref[...]
    rest = low_ref[...] + (mid_ref[...] + (cross + cross.T))
    high, low = two_sum(high_ref[...], rest)
    turned = last_ref[...].T
    end_high = turned[0:8]
    end_low = jnp.zeros_like(end_high)
    for row in range(8, 128, 8):
        end_high, error = two_sum(end_high, turned[row : row + 8])
        end_low = end_low + error
    row_high, row_low = end_high[0:1], end_low[0:1]
    for row in range(1, 8):
        row_high, error = two_sum(row_high, end_high[row : row + 1])
        row_low = row_low + (error + end_low[row : row + 1])
    even = even_core()
    for place, (gram, last) in enumerate(((high, row_high), (low, row_low))):
        packed = pack(gram, last)
        kept_ref[place] = jnp.where(even, packed[:HALF], packed[HALF:])
        sent_ref[place] = jnp.where(even, packed[HALF:], packed[:HALF])


def even_core():
    return lax.axis_index("space") % 2 == 0


def fetch(panel_ref, x_ref, sems, chunk, index):
    at = pl.ds(pl.multiple_of(index * chunk, chunk), chunk)
    return pltpu.make_async_copy(panel_ref.at[:, at], x_ref.at[:, at], sems.at[index])


def pack(gram, last):
    rows, lanes = iota((64, 128), 0), iota((64, 128), 1)
    turned = pltpu.roll(gram[64:128], 64, 1)
    folded = jnp.where(lanes > rows, gram[0:64], jnp.where(lanes < rows, turned, 0.0))
    on_diagonal = iota((128, 128), 0) == iota((128, 128), 1)
    diagonal = jnp.sum(jnp.where(on_diagonal, gram, 0.0), axis=0, keepdims=True)
    return jnp.concatenate([folded, diagonal, last, jnp.zeros((2 * HALF - 66, 128), F32)], axis=0)


def unpack(packed):
    rows, lanes = iota((64, 128), 0), iota((64, 128), 1)
    folded = packed[0:64]
    top = jnp.where(lanes > rows, folded, 0.0)
    turned = pltpu.roll(folded, 64, 1)
    bottom = jnp.where((lanes >= 64) & (lanes - 64 < rows), turned, 0.0)
    half = jnp.concatenate([top, bottom], axis=0)
    on_diagonal = iota((128, 128), 0) == iota((128, 128), 1)
    gram = jnp.where(on_diagonal, packed[64:65], half + half.T)
    return gram, packed[65:66]


def local_gram(panel, chunk=4096, part=1024):
    snaps, columns = panel.shape
    square = pltpu.VMEM((128, 128), F32)
    return pl.pallas_call(
        functools.partial(gram_body, chunk, part),
        in_specs=[pl.BlockSpec(memory_space=pl.ANY)],
        out_shape=[jax.ShapeDtypeStruct((2, HALF, 128), F32)] * 2,
        scratch_shapes=[pltpu.VMEM((snaps, columns), F32)]
        + [square] * 5
        + [pltpu.SemaphoreType.DMA((columns // chunk,))],
        compiler_params=pltpu.CompilerParams(vmem_limit_bytes=LIMIT),
        name="gram",
    )(panel)


def pair_add(a, b):
    total, rest = two_sum(a[0], b[0])
    return jnp.stack([total, (a[1] + b[1]) + rest])


def exchange(x, pairs):
    return lax.ppermute(x, "space", pairs)


def flips(size, step):
    return [(i, i ^ step) for i in range(size)]


def sum_pairs(kept, sent, size):
    half = pair_add(kept, exchange(sent, flips(size, 1)))
    for step in (2, 8):
        first = exchange(half, flips(size, step))
        second = exchange(half, flips(size, 2 * step))
        third = exchange(half, flips(size, 3 * step))
        half = pair_add(pair_add(half, first), pair_add(second, third))
    half = pair_add(half, exchange(half, flips(size, 32)))
    before = exchange(half, [(i, (i + 64) % size) for i in range(size)])
    after = exchange(half, [(i, (i - 64) % size) for i in range(size)])
    across = exchange(half, flips(size, 160))
    half = pair_add(pair_add(half, across), pair_add(before, after))
    return half, exchange(half, flips(size, 1))


def power_scale(square):
    scale = jnp.ones_like(square)
    inverse = jnp.ones_like(square)
    for k in (32, 16, 8, 4, 2, 1):
        big = square >= 4.0**k
        square = jnp.where(big, square * 4.0**-k, square)
        scale = jnp.where(big, scale * 2.0**-k, scale)
        inverse = jnp.where(big, inverse * 2.0**k, inverse)
    for k in (32, 16, 8, 4, 2, 1):
        small = square < 4.0 ** (1 - k)
        square = jnp.where(small, square * 4.0**k, square)
        scale = jnp.where(small, scale * 2.0**k, scale)
        inverse = jnp.where(small, inverse * 2.0**-k, inverse)
    return scale, inverse


def slices(high, low, unit, count):
    out = []
    rest = high
    for index in range(count):
        if index == 2 and low is not None:
            rest = rest + low
        magic = 1.5 * 2.0**23 * unit * 2.0 ** (-9 * index)
        piece = (rest + magic) - magic
        rest = rest - piece
        out.append(piece)
    return out


def add_levels(levels):
    total, rest = two_sum(levels[0], levels[1])
    for level in levels[2:4]:
        total, error = two_sum(total, level)
        rest = rest + error
    for level in levels[4:]:
        rest = rest + level
    return two_sum(total, rest)


def factor(matrix, size=16):
    count = 128 // size
    work = [matrix[size * i : size * i + size] for i in range(count)]
    lanes, rows = iota((size, 128), 1), iota((size, 128), 0)
    extra = [jnp.where(lanes == rows + size * i, 1.0, 0.0).astype(F32) for i in range(count)]
    upper, inverse = [], []
    for block in range(count):
        at = size * block
        wide, carried = work[block], extra[block]
        columns = [jnp.broadcast_to(wide[:, at + k : at + k + 1], (size, 128)) for k in range(size)]
        pivots = jnp.ones((size, 128), F32)
        for j in range(size):
            pivot = columns[j][j : j + 1]
            pivots = jnp.where(rows == j, jnp.broadcast_to(pivot, (size, 128)), pivots)
            if j == size - 1:
                break
            ratio = jnp.where(rows > j, columns[j] * jnp.broadcast_to(1.0 / pivot, (size, 128)), 0.0)
            for k in range(j + 1, size):
                columns[k] = columns[k] - ratio * jnp.broadcast_to(columns[k][j : j + 1], (size, 128))
            wide = wide - ratio * jnp.broadcast_to(wide[j : j + 1], (size, 128))
            carried = carried - ratio * jnp.broadcast_to(carried[j : j + 1], (size, 128))
        root = lax.rsqrt(pivots)
        root = root * (1.5 - 0.5 * pivots * root * root)
        wide = jnp.where(lanes >= rows + at, wide * root, 0.0)
        carried = carried * root
        upper.append(wide)
        inverse.append(carried)
        if block < count - 1:
            left = split3(wide)
            right = split3(jnp.concatenate([wide, carried], axis=1))
            order = ((0, 0), (0, 1), (1, 0), (1, 1), (0, 2), (2, 0))
            update = dot(
                jnp.concatenate([left[i] for i, _ in order], axis=0),
                jnp.concatenate([right[j] for _, j in order], axis=0),
                TN,
            )
            for later in range(block + 1, count):
                at = size * later
                work[later] = work[later] - update[at : at + size, :128]
                extra[later] = extra[later] - update[at : at + size, 128:]
    return jnp.concatenate(upper, axis=0), jnp.concatenate(inverse, axis=0)


def finish_body(
    root,
    chunk,
    out_chunk,
    mine_ref,
    other_ref,
    table_ref,
    index_ref,
    coef_ref,
    panel_ref,
    modes_ref,
    operator_ref,
    factor_ref,
    x_ref,
    y_ref,
    shift_ref,
    in_sems,
    out_sems,
):
    columns = panel_ref.shape[1]
    for index in range(columns // chunk):
        fetch(panel_ref, x_ref, in_sems, chunk, index).start()
    even = even_core()
    mine, other = mine_ref[...], other_ref[...]
    packed = jnp.concatenate([jnp.where(even, mine, other), jnp.where(even, other, mine)], axis=1)
    gram_high, last_high = unpack(packed[0])
    gram_low, last_low = unpack(packed[1])
    gram_high, gram_low = two_sum(gram_high, gram_low)
    last_high, last_low = two_sum(last_high, last_low)
    on_diagonal = iota((128, 128), 0) == iota((128, 128), 1)
    diagonal = jnp.sum(jnp.where(on_diagonal, gram_high, 0.0), axis=0, keepdims=True)
    scale, unscale = power_scale(diagonal)
    scale_wide = jnp.broadcast_to(scale, (128, 128))
    scale_tall = scale_wide.T
    gram_high = gram_high * scale_wide * scale_tall
    gram_low = gram_low * scale_wide * scale_tall
    last_high = last_high * scale
    last_low = last_low * scale
    biggest = jnp.max(jnp.abs(last_high), axis=1, keepdims=True)
    last_scale, last_unscale = power_scale(jnp.broadcast_to(biggest * biggest, (1, 128)))
    last_high = last_high * last_scale
    last_low = last_low * last_scale

    upper, lower_inverse = factor(gram_high)
    factor_ref[...] = upper * (unscale * (1.0 / root))

    norms = jnp.sum(lower_inverse * lower_inverse, axis=1, keepdims=True)
    row_scale, _ = power_scale(jnp.broadcast_to(norms, (128, 128)))
    y_one, y_two = slices(lower_inverse * row_scale, None, 2.0**-7, 2)
    first = y_one + y_two
    y_both = jnp.concatenate([y_one, y_two], axis=0).astype(BF16)

    blank = jnp.zeros((7, 128), F32)
    whole_high = jnp.concatenate([gram_high, last_high, blank], axis=0)
    whole_low = jnp.concatenate([gram_low, last_low, blank], axis=0)
    g = [piece.astype(BF16) for piece in slices(whole_high, whole_low, 2.0**-6, 4)]
    p = [dot(piece, y_both, NT) for piece in g]
    one = [piece[:, :128] for piece in p]
    two = [piece[:, 128:] for piece in p]
    t_high, t_low = add_levels(
        [one[0], one[1] + two[0], one[2] + two[1], one[3] + two[2], two[3]]
    )

    norms = jnp.sum(t_high[:128] * t_high[:128], axis=0, keepdims=True)
    column_scale, column_unscale = power_scale(norms)
    t = slices(t_high[:128] * column_scale, t_low[:128] * column_scale, 2.0**-7, 4)
    t_all = jnp.concatenate([piece.astype(BF16) for piece in t], axis=1)
    s = dot(y_both, t_all, NN)
    one = [s[:128, 128 * k : 128 * k + 128] for k in range(4)]
    two = [s[128:, 128 * k : 128 * k + 128] for k in range(4)]
    s_high, s_low = add_levels(
        [one[0], one[1] + two[0], one[2] + two[1], one[3] + two[2], two[3]]
    )
    _, second = factor((s_high + s_low) * column_unscale)

    whole = dot(second, first, NN, HIGH)
    shift_ref[...] = t_high
    z = shift_ref[1:129]
    following = jnp.where(iota((1, 128), 1) == 127, last_unscale, pltpu.roll(unscale, 127, 1))
    h = dot(whole * (scale * following), z, NN, HIGH)
    operator_ref[...] = dot(second, h, NT, HIGH)

    rows = iota((16, 128), 0)
    index, coef = jnp.zeros((16, 128), jnp.int32), jnp.zeros((16, 128), F32)
    for mode in range(16):
        index = jnp.where(rows == mode, index_ref[mode], index)
        coef = jnp.where(rows == mode, coef_ref[mode], coef)
    onehot = (iota((16, 128), 1) == index).astype(F32)
    chosen = dot(onehot, table_ref[...], NT, HIGH)
    comb = dot(chosen, whole, NN, HIGH) * scale * (coef * root)

    for index in range(columns // chunk):
        fetch(panel_ref, x_ref, in_sems, chunk, index).wait()
    shifted = jnp.where(iota(comb.shape, 1) == 0, 0.0, pltpu.roll(comb, 1, 1))
    c = split3(shifted)
    left = jnp.concatenate(
        [
            jnp.concatenate([c[0], c[1]], axis=1),
            jnp.concatenate([c[1], c[0]], axis=1),
            jnp.concatenate([c[2], jnp.zeros_like(c[2])], axis=1),
        ],
        axis=0,
    )

    def send(index):
        at = pl.ds(pl.multiple_of(index * out_chunk, out_chunk), out_chunk)
        return pltpu.make_async_copy(y_ref.at[:, at], modes_ref.at[:, at], out_sems.at[index])

    def step(index, carry):
        at = pl.ds(pl.multiple_of(index * out_chunk, out_chunk), out_chunk)
        x_high, x_mid, x_low = split3(x_ref[0:128, at])
        main = dot(left, jnp.concatenate([x_high, x_mid], axis=0), NN)
        side = dot(c[0], x_low, NN)
        end = comb[:, 127:128] * x_ref[128:129, at]
        y_ref[:, at] = (main[0:16] + end) + (main[16:32] + (main[32:48] + side))
        send(index).start()
        return carry

    lax.fori_loop(0, columns // out_chunk, step, 0)
    for index in range(columns // out_chunk):
        send(index).wait()


def finish(mine, other, table, index, coef, panel, total_rows, chunk=4096, out_chunk=2048):
    root = float(total_rows) ** 0.5
    modes = index.shape[0]
    snaps, columns = panel.shape
    whole = pl.BlockSpec(memory_space=pltpu.VMEM)
    remote = pl.BlockSpec(memory_space=pl.ANY)
    scalars = pl.BlockSpec(memory_space=pltpu.SMEM)
    return pl.pallas_call(
        functools.partial(finish_body, root, chunk, out_chunk),
        in_specs=[whole] * 3 + [scalars] * 2 + [remote],
        out_specs=[remote, whole, whole],
        out_shape=[
            jax.ShapeDtypeStruct((modes, columns), F32),
            jax.ShapeDtypeStruct((128, 128), F32),
            jax.ShapeDtypeStruct((128, 128), F32),
        ],
        scratch_shapes=[
            pltpu.VMEM((snaps, columns), F32),
            pltpu.VMEM((modes, columns), F32),
            pltpu.VMEM((136, 128), F32),
            pltpu.SemaphoreType.DMA((columns // chunk,)),
            pltpu.SemaphoreType.DMA((columns // out_chunk,)),
        ],
        compiler_params=pltpu.CompilerParams(vmem_limit_bytes=LIMIT),
        name="finish",
    )(mine, other, table, index, coef, panel)


def local(size, panel, eig_table, mode_index, mode_coef):
    mine, other = sum_pairs(*local_gram(panel), size)
    return tuple(finish(mine, other, eig_table, mode_index, mode_coef, panel, panel.shape[1] * size))


def solution(mesh):
    return jax.shard_map(
        functools.partial(local, mesh.shape["space"]),
        mesh=mesh,
        in_specs=(P(None, "space"), P(), P(), P()),
        out_specs=(P(None, "space"), P(), P()),
        check_vma=False,
    )
```

```python
import functools

import jax
import jax.numpy as jnp
from jax import lax
from jax.experimental import pallas as pl
from jax.experimental.pallas import tpu as pltpu
from jax.sharding import PartitionSpec as P

HIGH = lax.Precision.HIGHEST
F32 = jnp.float32
BF16 = jnp.bfloat16
NT = (((1,), (1,)), ((), ()))
NN = (((1,), (0,)), ((), ()))
TN = (((0,), (0,)), ((), ()))
HALF = 40
GRAM_LIMIT = 50 * 1024 * 1024
LIMIT = 32 * 1024 * 1024


def dot(a, b, dims, precision=None):
    return lax.dot_general(a, b, dims, precision=precision, preferred_element_type=F32)


def two_sum(a, b):
    total = a + b
    other = total - a
    return total, (a - (total - other)) + (b - other)


def split3(x):
    high = x.astype(BF16)
    rest = x - high.astype(F32)
    mid = rest.astype(BF16)
    return high, mid, (rest - mid.astype(F32)).astype(BF16)


def iota(shape, axis):
    return lax.broadcasted_iota(jnp.int32, shape, axis)


def gram_body(chunk, part, panel_ref, kept_ref, sent_ref, x_ref, high_ref, low_ref, cross_ref, mid_ref, last_ref, sems):
    count = panel_ref.shape[1] // chunk
    for index in range(count):
        fetch(panel_ref, x_ref, sems, chunk, index).start()
    for ref in (high_ref, low_ref, cross_ref, mid_ref, last_ref):
        ref[...] = jnp.zeros_like(ref)

    def step(index, carry):
        fetch(panel_ref, x_ref, sems, chunk, index).wait()
        for start in range(0, chunk, part):
            at = pl.ds(pl.multiple_of(index * chunk + start, part), part)
            x = x_ref[0:128, at]
            high, mid, low = split3(x)
            main = dot(jnp.concatenate([high, low], axis=0), jnp.concatenate([high, mid], axis=0), NT)
            total, rest = two_sum(high_ref[...], main[:128, :128])
            high_ref[...] = total
            low_ref[...] += rest
            cross_ref[...] += main[:128, 128:] + (main[128:, :128] + main[128:, 128:])
            mid_ref[...] += dot(mid, mid, NT)
            end = x_ref[128:129, at]
            partial = x[:, 0:128] * end[:, 0:128]
            for tile in range(128, part, 128):
                partial = partial + x[:, tile : tile + 128] * end[:, tile : tile + 128]
            last_ref[...] += partial
        return carry

    lax.fori_loop(0, count, step, 0)
    cross = cross_ref[...]
    rest = low_ref[...] + (mid_ref[...] + (cross + cross.T))
    high, low = two_sum(high_ref[...], rest)
    turned = last_ref[...].T
    end_high = turned[0:8]
    end_low = jnp.zeros_like(end_high)
    for row in range(8, 128, 8):
        end_high, error = two_sum(end_high, turned[row : row + 8])
        end_low = end_low + error
    row_high, row_low = end_high[0:1], end_low[0:1]
    for row in range(1, 8):
        row_high, error = two_sum(row_high, end_high[row : row + 1])
        row_low = row_low + (error + end_low[row : row + 1])
    even = even_core()
    for place, (gram, last) in enumerate(((high, row_high), (low, row_low))):
        packed = pack(gram, last)
        kept_ref[place] = jnp.where(even, packed[:HALF], packed[HALF:])
        sent_ref[place] = jnp.where(even, packed[HALF:], packed[:HALF])


def even_core():
    return lax.axis_index("space") % 2 == 0


def fetch(panel_ref, x_ref, sems, chunk, index):
    at = pl.ds(pl.multiple_of(index * chunk, chunk), chunk)
    return pltpu.make_async_copy(panel_ref.at[:, at], x_ref.at[:, at], sems.at[index])


def pack(gram, last):
    rows, lanes = iota((64, 128), 0), iota((64, 128), 1)
    turned = pltpu.roll(gram[64:128], 64, 1)
    folded = jnp.where(lanes > rows, gram[0:64], jnp.where(lanes < rows, turned, 0.0))
    on_diagonal = iota((128, 128), 0) == iota((128, 128), 1)
    diagonal = jnp.sum(jnp.where(on_diagonal, gram, 0.0), axis=0, keepdims=True)
    return jnp.concatenate([folded, diagonal, last, jnp.zeros((2 * HALF - 66, 128), F32)], axis=0)


def unpack(packed):
    rows, lanes = iota((64, 128), 0), iota((64, 128), 1)
    folded = packed[0:64]
    top = jnp.where(lanes > rows, folded, 0.0)
    turned = pltpu.roll(folded, 64, 1)
    bottom = jnp.where((lanes >= 64) & (lanes - 64 < rows), turned, 0.0)
    half = jnp.concatenate([top, bottom], axis=0)
    on_diagonal = iota((128, 128), 0) == iota((128, 128), 1)
    gram = jnp.where(on_diagonal, packed[64:65], half + half.T)
    return gram, packed[65:66]


def local_gram(panel, chunk=4096, part=1024):
    snaps, columns = panel.shape
    square = pltpu.VMEM((128, 128), F32)
    return pl.pallas_call(
        functools.partial(gram_body, chunk, part),
        in_specs=[pl.BlockSpec(memory_space=pl.ANY)],
        out_shape=[pltpu.VMEM((2, HALF, 128), F32)] * 2 + [pltpu.VMEM((snaps, columns), F32)],
        out_specs=[pl.BlockSpec(memory_space=pltpu.VMEM)] * 3,
        scratch_shapes=[square] * 5
        + [pltpu.SemaphoreType.DMA((columns // chunk,))],
        compiler_params=pltpu.CompilerParams(vmem_limit_bytes=GRAM_LIMIT),
        name="gram",
    )(panel)


def pair_add(a, b):
    total, rest = two_sum(a[0], b[0])
    return jnp.stack([total, (a[1] + b[1]) + rest])


def exchange(x, pairs):
    return lax.ppermute(x, "space", pairs)


def flips(size, step):
    return [(i, i ^ step) for i in range(size)]


def sum_pairs(kept, sent, size):
    half = pair_add(kept, exchange(sent, flips(size, 1)))
    for step in (2, 8):
        first = exchange(half, flips(size, step))
        second = exchange(half, flips(size, 2 * step))
        third = exchange(half, flips(size, 3 * step))
        half = pair_add(pair_add(half, first), pair_add(second, third))
    half = pair_add(half, exchange(half, flips(size, 32)))
    before = exchange(half, [(i, (i + 64) % size) for i in range(size)])
    after = exchange(half, [(i, (i - 64) % size) for i in range(size)])
    across = exchange(half, flips(size, 160))
    half = pair_add(pair_add(half, across), pair_add(before, after))
    return half, exchange(half, flips(size, 1))


def power_scale(square):
    scale = jnp.ones_like(square)
    inverse = jnp.ones_like(square)
    for k in (32, 16, 8, 4, 2, 1):
        big = square >= 4.0**k
        square = jnp.where(big, square * 4.0**-k, square)
        scale = jnp.where(big, scale * 2.0**-k, scale)
        inverse = jnp.where(big, inverse * 2.0**k, inverse)
    for k in (32, 16, 8, 4, 2, 1):
        small = square < 4.0 ** (1 - k)
        square = jnp.where(small, square * 4.0**k, square)
        scale = jnp.where(small, scale * 2.0**k, scale)
        inverse = jnp.where(small, inverse * 2.0**-k, inverse)
    return scale, inverse


def slices(high, low, unit, count):
    out = []
    rest = high
    for index in range(count):
        if index == 2 and low is not None:
            rest = rest + low
        magic = 1.5 * 2.0**23 * unit * 2.0 ** (-9 * index)
        piece = (rest + magic) - magic
        rest = rest - piece
        out.append(piece)
    return out


def add_levels(levels):
    total, rest = two_sum(levels[0], levels[1])
    for level in levels[2:4]:
        total, error = two_sum(total, level)
        rest = rest + error
    for level in levels[4:]:
        rest = rest + level
    return two_sum(total, rest)


def factor(matrix, size=16):
    count = 128 // size
    work = [matrix[size * i : size * i + size] for i in range(count)]
    lanes, rows = iota((size, 128), 1), iota((size, 128), 0)
    extra = [jnp.where(lanes == rows + size * i, 1.0, 0.0).astype(F32) for i in range(count)]
    upper, inverse = [], []
    for block in range(count):
        at = size * block
        wide, carried = work[block], extra[block]
        columns = [jnp.broadcast_to(wide[:, at + k : at + k + 1], (size, 128)) for k in range(size)]
        pivots = jnp.ones((size, 128), F32)
        for j in range(size):
            pivot = columns[j][j : j + 1]
            pivots = jnp.where(rows == j, jnp.broadcast_to(pivot, (size, 128)), pivots)
            if j == size - 1:
                break
            ratio = jnp.where(rows > j, columns[j] * jnp.broadcast_to(1.0 / pivot, (size, 128)), 0.0)
            for k in range(j + 1, size):
                columns[k] = columns[k] - ratio * jnp.broadcast_to(columns[k][j : j + 1], (size, 128))
            wide = wide - ratio * jnp.broadcast_to(wide[j : j + 1], (size, 128))
            carried = carried - ratio * jnp.broadcast_to(carried[j : j + 1], (size, 128))
        root = lax.rsqrt(pivots)
        root = root * (1.5 - 0.5 * pivots * root * root)
        wide = jnp.where(lanes >= rows + at, wide * root, 0.0)
        carried = carried * root
        upper.append(wide)
        inverse.append(carried)
        if block < count - 1:
            left = split3(wide)
            right = split3(jnp.concatenate([wide, carried], axis=1))
            order = ((0, 0), (0, 1), (1, 0), (1, 1), (0, 2), (2, 0))
            update = dot(
                jnp.concatenate([left[i] for i, _ in order], axis=0),
                jnp.concatenate([right[j] for _, j in order], axis=0),
                TN,
            )
            for later in range(block + 1, count):
                at = size * later
                work[later] = work[later] - update[at : at + size, :128]
                extra[later] = extra[later] - update[at : at + size, 128:]
    return jnp.concatenate(upper, axis=0), jnp.concatenate(inverse, axis=0)


def finish_body(
    root,
    out_chunk,
    mine_ref,
    other_ref,
    table_ref,
    index_ref,
    coef_ref,
    x_ref,
    modes_ref,
    operator_ref,
    factor_ref,
    y_ref,
    shift_ref,
    out_sems,
):
    columns = x_ref.shape[1]
    even = even_core()
    mine, other = mine_ref[...], other_ref[...]
    packed = jnp.concatenate([jnp.where(even, mine, other), jnp.where(even, other, mine)], axis=1)
    gram_high, last_high = unpack(packed[0])
    gram_low, last_low = unpack(packed[1])
    gram_high, gram_low = two_sum(gram_high, gram_low)
    last_high, last_low = two_sum(last_high, last_low)
    on_diagonal = iota((128, 128), 0) == iota((128, 128), 1)
    diagonal = jnp.sum(jnp.where(on_diagonal, gram_high, 0.0), axis=0, keepdims=True)
    scale, unscale = power_scale(diagonal)
    scale_wide = jnp.broadcast_to(scale, (128, 128))
    scale_tall = scale_wide.T
    gram_high = gram_high * scale_wide * scale_tall
    gram_low = gram_low * scale_wide * scale_tall
    last_high = last_high * scale
    last_low = last_low * scale
    biggest = jnp.max(jnp.abs(last_high), axis=1, keepdims=True)
    last_scale, last_unscale = power_scale(jnp.broadcast_to(biggest * biggest, (1, 128)))
    last_high = last_high * last_scale
    last_low = last_low * last_scale

    upper, lower_inverse = factor(gram_high)
    factor_ref[...] = upper * (unscale * (1.0 / root))

    norms = jnp.sum(lower_inverse * lower_inverse, axis=1, keepdims=True)
    row_scale, _ = power_scale(jnp.broadcast_to(norms, (128, 128)))
    y_one, y_two = slices(lower_inverse * row_scale, None, 2.0**-7, 2)
    first = y_one + y_two
    y_both = jnp.concatenate([y_one, y_two], axis=0).astype(BF16)

    blank = jnp.zeros((7, 128), F32)
    whole_high = jnp.concatenate([gram_high, last_high, blank], axis=0)
    whole_low = jnp.concatenate([gram_low, last_low, blank], axis=0)
    g = [piece.astype(BF16) for piece in slices(whole_high, whole_low, 2.0**-6, 4)]
    p = [dot(piece, y_both, NT) for piece in g]
    one = [piece[:, :128] for piece in p]
    two = [piece[:, 128:] for piece in p]
    t_high, t_low = add_levels(
        [one[0], one[1] + two[0], one[2] + two[1], one[3] + two[2], two[3]]
    )

    norms = jnp.sum(t_high[:128] * t_high[:128], axis=0, keepdims=True)
    column_scale, column_unscale = power_scale(norms)
    t = slices(t_high[:128] * column_scale, t_low[:128] * column_scale, 2.0**-7, 4)
    t_all = jnp.concatenate([piece.astype(BF16) for piece in t], axis=1)
    s = dot(y_both, t_all, NN)
    one = [s[:128, 128 * k : 128 * k + 128] for k in range(4)]
    two = [s[128:, 128 * k : 128 * k + 128] for k in range(4)]
    s_high, s_low = add_levels(
        [one[0], one[1] + two[0], one[2] + two[1], one[3] + two[2], two[3]]
    )
    _, second = factor((s_high + s_low) * column_unscale)

    whole = dot(second, first, NN, HIGH)
    shift_ref[...] = t_high
    z = shift_ref[1:129]
    following = jnp.where(iota((1, 128), 1) == 127, last_unscale, pltpu.roll(unscale, 127, 1))
    h = dot(whole * (scale * following), z, NN, HIGH)
    operator_ref[...] = dot(second, h, NT, HIGH)

    rows = iota((16, 128), 0)
    index, coef = jnp.zeros((16, 128), jnp.int32), jnp.zeros((16, 128), F32)
    for mode in range(16):
        index = jnp.where(rows == mode, index_ref[mode], index)
        coef = jnp.where(rows == mode, coef_ref[mode], coef)
    onehot = (iota((16, 128), 1) == index).astype(F32)
    chosen = dot(onehot, table_ref[...], NT, HIGH)
    comb = dot(chosen, whole, NN, HIGH) * scale * (coef * root)

    shifted = jnp.where(iota(comb.shape, 1) == 0, 0.0, pltpu.roll(comb, 1, 1))
    c = split3(shifted)
    left = jnp.concatenate(
        [
            jnp.concatenate([c[0], c[1]], axis=1),
            jnp.concatenate([c[1], c[0]], axis=1),
            jnp.concatenate([c[2], jnp.zeros_like(c[2])], axis=1),
        ],
        axis=0,
    )

    def send(index):
        at = pl.ds(pl.multiple_of(index * out_chunk, out_chunk), out_chunk)
        return pltpu.make_async_copy(y_ref.at[:, at], modes_ref.at[:, at], out_sems.at[index])

    def step(index, carry):
        at = pl.ds(pl.multiple_of(index * out_chunk, out_chunk), out_chunk)
        x_high, x_mid, x_low = split3(x_ref[0:128, at])
        main = dot(left, jnp.concatenate([x_high, x_mid], axis=0), NN)
        side = dot(c[0], x_low, NN)
        end = comb[:, 127:128] * x_ref[128:129, at]
        y_ref[:, at] = (main[0:16] + end) + (main[16:32] + (main[32:48] + side))
        send(index).start()
        return carry

    lax.fori_loop(0, columns // out_chunk, step, 0)
    for index in range(columns // out_chunk):
        send(index).wait()


def finish(mine, other, table, index, coef, panel, total_rows, out_chunk=2048):
    root = float(total_rows) ** 0.5
    modes = index.shape[0]
    columns = panel.shape[1]
    whole = pl.BlockSpec(memory_space=pltpu.VMEM)
    remote = pl.BlockSpec(memory_space=pl.ANY)
    scalars = pl.BlockSpec(memory_space=pltpu.SMEM)
    return pl.pallas_call(
        functools.partial(finish_body, root, out_chunk),
        in_specs=[whole] * 3 + [scalars] * 2 + [whole],
        out_specs=[remote, whole, whole],
        out_shape=[
            jax.ShapeDtypeStruct((modes, columns), F32),
            jax.ShapeDtypeStruct((128, 128), F32),
            jax.ShapeDtypeStruct((128, 128), F32),
        ],
        scratch_shapes=[
            pltpu.VMEM((modes, columns), F32),
            pltpu.VMEM((136, 128), F32),
            pltpu.SemaphoreType.DMA((columns // out_chunk,)),
        ],
        compiler_params=pltpu.CompilerParams(vmem_limit_bytes=LIMIT),
        name="finish",
    )(mine, other, table, index, coef, panel)


def local(size, panel, eig_table, mode_index, mode_coef):
    kept, sent, held = local_gram(panel)
    mine, other = sum_pairs(kept, sent, size)
    return tuple(finish(mine, other, eig_table, mode_index, mode_coef, held, panel.shape[1] * size))


def solution(mesh):
    return jax.shard_map(
        functools.partial(local, mesh.shape["space"]),
        mesh=mesh,
        in_specs=(P(None, "space"), P(), P(), P()),
        out_specs=(P(None, "space"), P(), P()),
        check_vma=False,
    )
```

```python
import functools

import jax
import jax.numpy as jnp
from jax import lax
from jax.experimental import pallas as pl
from jax.experimental.pallas import tpu as pltpu
from jax.sharding import PartitionSpec as P

HIGH = lax.Precision.HIGHEST
F32 = jnp.float32
BF16 = jnp.bfloat16
NT = (((1,), (1,)), ((), ()))
NN = (((1,), (0,)), ((), ()))
TN = (((0,), (0,)), ((), ()))
HALF = 40
GRAM_LIMIT = 50 * 1024 * 1024
LIMIT = 32 * 1024 * 1024


def dot(a, b, dims, precision=None):
    return lax.dot_general(a, b, dims, precision=precision, preferred_element_type=F32)


def two_sum(a, b):
    total = a + b
    other = total - a
    return total, (a - (total - other)) + (b - other)


def split3(x):
    high = x.astype(BF16)
    rest = x - high.astype(F32)
    mid = rest.astype(BF16)
    return high, mid, (rest - mid.astype(F32)).astype(BF16)


def iota(shape, axis):
    return lax.broadcasted_iota(jnp.int32, shape, axis)


def gram_body(
    chunk,
    part,
    panel_ref,
    kept_ref,
    sent_ref,
    x_ref,
    high_ref,
    low_ref,
    cross_ref,
    mid_ref,
    last_ref,
    sems,
):
    count = panel_ref.shape[1] // chunk
    for index in range(count):
        fetch(panel_ref, x_ref, sems, chunk, index).start()
    for ref in (high_ref, low_ref, cross_ref, mid_ref, last_ref):
        ref[...] = jnp.zeros_like(ref)

    def step(index, carry):
        fetch(panel_ref, x_ref, sems, chunk, index).wait()
        for start in range(0, chunk, part):
            at = pl.ds(pl.multiple_of(index * chunk + start, part), part)
            x = x_ref[0:128, at]
            high, mid, low = split3(x)
            main = dot(jnp.concatenate([high, low], axis=0), jnp.concatenate([high, mid], axis=0), NT)
            total, rest = two_sum(high_ref[...], main[:128, :128])
            high_ref[...] = total
            low_ref[...] += rest
            cross_ref[...] += main[:128, 128:] + (main[128:, :128] + main[128:, 128:])
            mid_ref[...] += dot(mid, mid, NT)
            end = x_ref[128:129, at]
            partial = x[:, 0:128] * end[:, 0:128]
            for tile in range(128, part, 128):
                partial = partial + x[:, tile : tile + 128] * end[:, tile : tile + 128]
            last_ref[...] += partial
        return carry

    lax.fori_loop(0, count, step, 0)
    cross = cross_ref[...]
    rest = low_ref[...] + (mid_ref[...] + (cross + cross.T))
    high, low = two_sum(high_ref[...], rest)
    turned = last_ref[...].T
    end_high = turned[0:8]
    end_low = jnp.zeros_like(end_high)
    for row in range(8, 128, 8):
        end_high, error = two_sum(end_high, turned[row : row + 8])
        end_low = end_low + error
    row_high, row_low = end_high[0:1], end_low[0:1]
    for row in range(1, 8):
        row_high, error = two_sum(row_high, end_high[row : row + 1])
        row_low = row_low + (error + end_low[row : row + 1])
    even = even_core()
    for place, (gram, last) in enumerate(((high, row_high), (low, row_low))):
        packed = pack(gram, last)
        kept_ref[place] = jnp.where(even, packed[:HALF], packed[HALF:])
        sent_ref[place] = jnp.where(even, packed[HALF:], packed[:HALF])


def even_core():
    return lax.axis_index("space") % 2 == 0


def fetch(panel_ref, x_ref, sems, chunk, index):
    at = pl.ds(pl.multiple_of(index * chunk, chunk), chunk)
    return pltpu.make_async_copy(panel_ref.at[:, at], x_ref.at[:, at], sems.at[index])


def pack(gram, last):
    rows, lanes = iota((64, 128), 0), iota((64, 128), 1)
    turned = pltpu.roll(gram[64:128], 64, 1)
    folded = jnp.where(lanes > rows, gram[0:64], jnp.where(lanes < rows, turned, 0.0))
    on_diagonal = iota((128, 128), 0) == iota((128, 128), 1)
    diagonal = jnp.sum(jnp.where(on_diagonal, gram, 0.0), axis=0, keepdims=True)
    return jnp.concatenate([folded, diagonal, last, jnp.zeros((2 * HALF - 66, 128), F32)], axis=0)


def unpack(packed):
    rows, lanes = iota((64, 128), 0), iota((64, 128), 1)
    folded = packed[0:64]
    top = jnp.where(lanes > rows, folded, 0.0)
    turned = pltpu.roll(folded, 64, 1)
    bottom = jnp.where((lanes >= 64) & (lanes - 64 < rows), turned, 0.0)
    half = jnp.concatenate([top, bottom], axis=0)
    on_diagonal = iota((128, 128), 0) == iota((128, 128), 1)
    gram = jnp.where(on_diagonal, packed[64:65], half + half.T)
    return gram, packed[65:66]


def local_gram(panel, chunk=4096, part=1024):
    snaps, columns = panel.shape
    square = pltpu.VMEM((128, 128), F32)
    return pl.pallas_call(
        functools.partial(gram_body, chunk, part),
        in_specs=[pl.BlockSpec(memory_space=pl.ANY)],
        out_shape=[pltpu.VMEM((2, HALF, 128), F32)] * 2
        + [pltpu.VMEM((snaps, columns), F32)],
        out_specs=[pl.BlockSpec(memory_space=pltpu.VMEM)] * 3,
        scratch_shapes=[square] * 5
        + [pltpu.SemaphoreType.DMA((columns // chunk,))],
        compiler_params=pltpu.CompilerParams(vmem_limit_bytes=GRAM_LIMIT),
        name="gram",
    )(panel)


def pair_add(a, b):
    total, rest = two_sum(a[0], b[0])
    return jnp.stack([total, (a[1] + b[1]) + rest])


def exchange(x, pairs):
    return lax.ppermute(x, "space", pairs)


def flips(size, step):
    return [(i, i ^ step) for i in range(size)]


def sum_pairs(kept, sent, size):
    half = pair_add(kept, exchange(sent, flips(size, 1)))
    for step in (2, 8, 32):
        first = exchange(half, flips(size, step))
        second = exchange(half, flips(size, 2 * step))
        third = exchange(half, flips(size, 3 * step))
        half = pair_add(pair_add(half, first), pair_add(second, third))
    half = pair_add(half, exchange(half, flips(size, 224)))
    return half, exchange(half, flips(size, 1))


def power_scale(square):
    scale = jnp.ones_like(square)
    inverse = jnp.ones_like(square)
    for k in (32, 16, 8, 4, 2, 1):
        big = square >= 4.0**k
        square = jnp.where(big, square * 4.0**-k, square)
        scale = jnp.where(big, scale * 2.0**-k, scale)
        inverse = jnp.where(big, inverse * 2.0**k, inverse)
    for k in (32, 16, 8, 4, 2, 1):
        small = square < 4.0 ** (1 - k)
        square = jnp.where(small, square * 4.0**k, square)
        scale = jnp.where(small, scale * 2.0**k, scale)
        inverse = jnp.where(small, inverse * 2.0**-k, inverse)
    return scale, inverse


def slices(high, low, unit, count):
    out = []
    rest = high
    for index in range(count):
        if index == 2 and low is not None:
            rest = rest + low
        magic = 1.5 * 2.0**23 * unit * 2.0 ** (-9 * index)
        piece = (rest + magic) - magic
        rest = rest - piece
        out.append(piece)
    return out


def add_levels(levels):
    total, rest = two_sum(levels[0], levels[1])
    for level in levels[2:4]:
        total, error = two_sum(total, level)
        rest = rest + error
    for level in levels[4:]:
        rest = rest + level
    return two_sum(total, rest)


def factor(matrix, size=16):
    count = 128 // size
    work = [matrix[size * i : size * i + size] for i in range(count)]
    lanes, rows = iota((size, 128), 1), iota((size, 128), 0)
    extra = [jnp.where(lanes == rows + size * i, 1.0, 0.0).astype(F32) for i in range(count)]
    upper, inverse = [], []
    for block in range(count):
        at = size * block
        wide, carried = work[block], extra[block]
        columns = [jnp.broadcast_to(wide[:, at + k : at + k + 1], (size, 128)) for k in range(size)]
        pivots = jnp.ones((size, 128), F32)
        for j in range(size):
            pivot = columns[j][j : j + 1]
            pivots = jnp.where(rows == j, jnp.broadcast_to(pivot, (size, 128)), pivots)
            if j == size - 1:
                break
            ratio = jnp.where(rows > j, columns[j] * jnp.broadcast_to(1.0 / pivot, (size, 128)), 0.0)
            for k in range(j + 1, size):
                columns[k] = columns[k] - ratio * jnp.broadcast_to(columns[k][j : j + 1], (size, 128))
            wide = wide - ratio * jnp.broadcast_to(wide[j : j + 1], (size, 128))
            carried = carried - ratio * jnp.broadcast_to(carried[j : j + 1], (size, 128))
        root = lax.rsqrt(pivots)
        root = root * (1.5 - 0.5 * pivots * root * root)
        wide = jnp.where(lanes >= rows + at, wide * root, 0.0)
        carried = carried * root
        upper.append(wide)
        inverse.append(carried)
        if block < count - 1:
            left = split3(wide)
            right = split3(jnp.concatenate([wide, carried], axis=1))
            order = ((0, 0), (0, 1), (1, 0), (1, 1), (0, 2), (2, 0))
            update = dot(
                jnp.concatenate([left[i] for i, _ in order], axis=0),
                jnp.concatenate([right[j] for _, j in order], axis=0),
                TN,
            )
            for later in range(block + 1, count):
                at = size * later
                work[later] = work[later] - update[at : at + size, :128]
                extra[later] = extra[later] - update[at : at + size, 128:]
    return jnp.concatenate(upper, axis=0), jnp.concatenate(inverse, axis=0)


def finish_body(
    root,
    out_chunk,
    mine_ref,
    other_ref,
    table_ref,
    index_ref,
    coef_ref,
    x_ref,
    modes_ref,
    operator_ref,
    factor_ref,
    y_ref,
    shift_ref,
    small_ref,
    small_sems,
    out_sems,
):
    columns = x_ref.shape[1]
    own = iota((16, 16), 0) == iota((16, 16), 1)
    index = jnp.sum(jnp.where(own, index_ref[...], 0), axis=1, keepdims=True)
    coef = jnp.sum(jnp.where(own, coef_ref[...], 0.0), axis=1, keepdims=True)
    onehot = (iota((16, 128), 1) == index).astype(F32)
    chosen = dot(onehot, table_ref[...], NT, HIGH) * (coef * root)
    even = even_core()
    mine, other = mine_ref[...], other_ref[...]
    packed = jnp.concatenate([jnp.where(even, mine, other), jnp.where(even, other, mine)], axis=1)
    gram_high, last_high = unpack(packed[0])
    gram_low, last_low = unpack(packed[1])
    gram_high, gram_low = two_sum(gram_high, gram_low)
    last_high, last_low = two_sum(last_high, last_low)
    on_diagonal = iota((128, 128), 0) == iota((128, 128), 1)
    diagonal = jnp.sum(jnp.where(on_diagonal, gram_high, 0.0), axis=0, keepdims=True)
    scale, unscale = power_scale(diagonal)
    scale_wide = jnp.broadcast_to(scale, (128, 128))
    scale_tall = scale_wide.T
    gram_high = gram_high * scale_wide * scale_tall
    gram_low = gram_low * scale_wide * scale_tall
    last_high = last_high * scale
    last_low = last_low * scale
    biggest = jnp.max(jnp.abs(last_high), axis=1, keepdims=True)
    last_scale, last_unscale = power_scale(jnp.broadcast_to(biggest * biggest, (1, 128)))
    last_high = last_high * last_scale
    last_low = last_low * last_scale

    upper, lower_inverse = factor(gram_high)
    small_ref[0] = upper * (unscale * (1.0 / root))
    factor_out = pltpu.make_async_copy(small_ref.at[0], factor_ref, small_sems.at[0])
    factor_out.start()

    norms = jnp.sum(lower_inverse * lower_inverse, axis=1, keepdims=True)
    row_scale, _ = power_scale(jnp.broadcast_to(norms, (128, 128)))
    y_one, y_two = slices(lower_inverse * row_scale, None, 2.0**-7, 2)
    first = y_one + y_two
    y_both = jnp.concatenate([y_one, y_two], axis=0).astype(BF16)

    blank = jnp.zeros((7, 128), F32)
    whole_high = jnp.concatenate([gram_high, last_high, blank], axis=0)
    whole_low = jnp.concatenate([gram_low, last_low, blank], axis=0)
    g = [piece.astype(BF16) for piece in slices(whole_high, whole_low, 2.0**-6, 4)]
    p = [dot(piece, y_both, NT) for piece in g]
    one = [piece[:, :128] for piece in p]
    two = [piece[:, 128:] for piece in p]
    t_high, t_low = add_levels(
        [one[0], one[1] + two[0], one[2] + two[1], one[3] + two[2], two[3]]
    )

    norms = jnp.sum(t_high[:128] * t_high[:128], axis=0, keepdims=True)
    column_scale, column_unscale = power_scale(norms)
    t = slices(t_high[:128] * column_scale, t_low[:128] * column_scale, 2.0**-7, 4)
    t_all = jnp.concatenate([piece.astype(BF16) for piece in t], axis=1)
    s = dot(y_both, t_all, NN)
    one = [s[:128, 128 * k : 128 * k + 128] for k in range(4)]
    two = [s[128:, 128 * k : 128 * k + 128] for k in range(4)]
    s_high, s_low = add_levels(
        [one[0], one[1] + two[0], one[2] + two[1], one[3] + two[2], two[3]]
    )
    _, second = factor((s_high + s_low) * column_unscale)

    whole = dot(second, first, NN, HIGH)
    shift_ref[...] = t_high
    z = shift_ref[1:129]
    following = jnp.where(iota((1, 128), 1) == 127, last_unscale, pltpu.roll(unscale, 127, 1))
    h = dot(whole * (scale * following), z, NN, HIGH)
    small_ref[1] = dot(second, h, NT, HIGH)
    operator_out = pltpu.make_async_copy(small_ref.at[1], operator_ref, small_sems.at[1])
    operator_out.start()
    comb = dot(chosen, whole, NN, HIGH) * scale

    shifted = jnp.where(iota(comb.shape, 1) == 0, 0.0, pltpu.roll(comb, 1, 1))
    c = split3(shifted)
    left = jnp.concatenate(
        [
            jnp.concatenate([c[0], c[1]], axis=1),
            jnp.concatenate([c[1], c[0]], axis=1),
            jnp.concatenate([c[2], jnp.zeros_like(c[2])], axis=1),
        ],
        axis=0,
    )

    def send(index):
        at = pl.ds(pl.multiple_of(index * out_chunk, out_chunk), out_chunk)
        return pltpu.make_async_copy(y_ref.at[:, at], modes_ref.at[:, at], out_sems.at[index])

    def step(index, carry):
        at = pl.ds(pl.multiple_of(index * out_chunk, out_chunk), out_chunk)
        x_high, x_mid, x_low = split3(x_ref[0:128, at])
        main = dot(left, jnp.concatenate([x_high, x_mid], axis=0), NN)
        side = dot(c[0], x_low, NN)
        end = comb[:, 127:128] * x_ref[128:129, at]
        y_ref[:, at] = (main[0:16] + end) + (main[16:32] + (main[32:48] + side))
        send(index).start()
        return carry

    lax.fori_loop(0, columns // out_chunk, step, 0)
    for index in range(columns // out_chunk):
        send(index).wait()
    factor_out.wait()
    operator_out.wait()


def finish(mine, other, table, index, coef, panel, root, out_chunk=4096):
    modes, columns = index.shape[0], panel.shape[1]
    whole = pl.BlockSpec(memory_space=pltpu.VMEM)
    remote = pl.BlockSpec(memory_space=pl.ANY)
    return pl.pallas_call(
        functools.partial(finish_body, root, out_chunk),
        in_specs=[whole] * 6,
        out_specs=[remote] * 3,
        out_shape=[
            jax.ShapeDtypeStruct((modes, columns), F32),
            jax.ShapeDtypeStruct((128, 128), F32),
            jax.ShapeDtypeStruct((128, 128), F32),
        ],
        scratch_shapes=[
            pltpu.VMEM((modes, columns), F32),
            pltpu.VMEM((136, 128), F32),
            pltpu.VMEM((2, 128, 128), F32),
            pltpu.SemaphoreType.DMA((2,)),
            pltpu.SemaphoreType.DMA((columns // out_chunk,)),
        ],
        compiler_params=pltpu.CompilerParams(vmem_limit_bytes=LIMIT),
        name="finish",
    )(mine, other, table, index.reshape(1, modes), coef.reshape(1, modes), panel)


def local(size, panel, eig_table, mode_index, mode_coef):
    root = float(panel.shape[1] * size) ** 0.5
    kept, sent, held = local_gram(panel)
    mine, other = sum_pairs(kept, sent, size)
    return tuple(finish(mine, other, eig_table, mode_index, mode_coef, held, root))


def solution(mesh):
    return jax.shard_map(
        functools.partial(local, mesh.shape["space"]),
        mesh=mesh,
        in_specs=(P(None, "space"), P(), P(), P()),
        out_specs=(P(None, "space"), P(), P()),
        check_vma=False,
    )
```

```python
import functools

import jax
import jax.numpy as jnp
from jax import lax
from jax.experimental import pallas as pl
from jax.experimental.pallas import tpu as pltpu
from jax.sharding import PartitionSpec as P

HIGH = lax.Precision.HIGHEST
F32 = jnp.float32
BF16 = jnp.bfloat16
NT = (((1,), (1,)), ((), ()))
NN = (((1,), (0,)), ((), ()))
TN = (((0,), (0,)), ((), ()))
HALF = 40
GRAM_LIMIT = 50 * 1024 * 1024
LIMIT = 32 * 1024 * 1024


def dot(a, b, dims, precision=None):
    return lax.dot_general(a, b, dims, precision=precision, preferred_element_type=F32)


def two_sum(a, b):
    total = a + b
    other = total - a
    return total, (a - (total - other)) + (b - other)


def split3(x):
    high = x.astype(BF16)
    rest = x - high.astype(F32)
    mid = rest.astype(BF16)
    return high, mid, (rest - mid.astype(F32)).astype(BF16)


def iota(shape, axis):
    return lax.broadcasted_iota(jnp.int32, shape, axis)


def gram_body(
    chunk,
    part,
    panel_ref,
    kept_ref,
    sent_ref,
    x_ref,
    high_ref,
    low_ref,
    cross_ref,
    mid_ref,
    last_ref,
    sems,
):
    count = panel_ref.shape[1] // chunk
    for index in range(count):
        fetch(panel_ref, x_ref, sems, chunk, index).start()
    for ref in (high_ref, low_ref, cross_ref, mid_ref, last_ref):
        ref[...] = jnp.zeros_like(ref)

    def step(index, carry):
        fetch(panel_ref, x_ref, sems, chunk, index).wait()
        for start in range(0, chunk, part):
            at = pl.ds(pl.multiple_of(index * chunk + start, part), part)
            x = x_ref[0:128, at]
            high, mid, low = split3(x)
            main = dot(jnp.concatenate([high, low], axis=0), jnp.concatenate([high, mid], axis=0), NT)
            total, rest = two_sum(high_ref[...], main[:128, :128])
            high_ref[...] = total
            low_ref[...] += rest
            cross_ref[...] += main[:128, 128:] + (main[128:, :128] + main[128:, 128:])
            mid_ref[...] += dot(mid, mid, NT)
            end = x_ref[128:129, at]
            partial = x[:, 0:128] * end[:, 0:128]
            for tile in range(128, part, 128):
                partial = partial + x[:, tile : tile + 128] * end[:, tile : tile + 128]
            last_ref[...] += partial
        return carry

    lax.fori_loop(0, count, step, 0)
    cross = cross_ref[...]
    rest = low_ref[...] + (mid_ref[...] + (cross + cross.T))
    high, low = two_sum(high_ref[...], rest)
    turned = last_ref[...].T
    end_high = turned[0:8]
    end_low = jnp.zeros_like(end_high)
    for row in range(8, 128, 8):
        end_high, error = two_sum(end_high, turned[row : row + 8])
        end_low = end_low + error
    row_high, row_low = end_high[0:1], end_low[0:1]
    for row in range(1, 8):
        row_high, error = two_sum(row_high, end_high[row : row + 1])
        row_low = row_low + (error + end_low[row : row + 1])
    even = even_core()
    for place, (gram, last) in enumerate(((high, row_high), (low, row_low))):
        packed = pack(gram, last)
        kept_ref[place] = jnp.where(even, packed[:HALF], packed[HALF:])
        sent_ref[place] = jnp.where(even, packed[HALF:], packed[:HALF])


def even_core():
    return lax.axis_index("space") % 2 == 0


def fetch(panel_ref, x_ref, sems, chunk, index):
    at = pl.ds(pl.multiple_of(index * chunk, chunk), chunk)
    return pltpu.make_async_copy(panel_ref.at[:, at], x_ref.at[:, at], sems.at[index])


def pack(gram, last):
    rows, lanes = iota((64, 128), 0), iota((64, 128), 1)
    turned = pltpu.roll(gram[64:128], 64, 1)
    folded = jnp.where(lanes > rows, gram[0:64], jnp.where(lanes < rows, turned, 0.0))
    on_diagonal = iota((128, 128), 0) == iota((128, 128), 1)
    diagonal = jnp.sum(jnp.where(on_diagonal, gram, 0.0), axis=0, keepdims=True)
    return jnp.concatenate([folded, diagonal, last, jnp.zeros((2 * HALF - 66, 128), F32)], axis=0)


def unpack(packed):
    rows, lanes = iota((64, 128), 0), iota((64, 128), 1)
    folded = packed[0:64]
    top = jnp.where(lanes > rows, folded, 0.0)
    turned = pltpu.roll(folded, 64, 1)
    bottom = jnp.where((lanes >= 64) & (lanes - 64 < rows), turned, 0.0)
    half = jnp.concatenate([top, bottom], axis=0)
    on_diagonal = iota((128, 128), 0) == iota((128, 128), 1)
    gram = jnp.where(on_diagonal, packed[64:65], half + half.T)
    return gram, packed[65:66]


def local_gram(panel, chunk=4096, part=1024):
    snaps, columns = panel.shape
    square = pltpu.VMEM((128, 128), F32)
    return pl.pallas_call(
        functools.partial(gram_body, chunk, part),
        in_specs=[pl.BlockSpec(memory_space=pl.ANY)],
        out_shape=[pltpu.VMEM((2, HALF, 128), F32)] * 2
        + [pltpu.VMEM((snaps, columns), F32)],
        out_specs=[pl.BlockSpec(memory_space=pltpu.VMEM)] * 3,
        scratch_shapes=[square] * 5
        + [pltpu.SemaphoreType.DMA((columns // chunk,))],
        compiler_params=pltpu.CompilerParams(vmem_limit_bytes=GRAM_LIMIT),
        name="gram",
    )(panel)


def pair_add(a, b):
    total, rest = two_sum(a[0], b[0])
    return jnp.stack([total, (a[1] + b[1]) + rest])


def exchange(x, pairs):
    return lax.ppermute(x, "space", pairs)


def flips(size, step):
    return [(i, i ^ step) for i in range(size)]


def sum_pairs(kept, sent, size):
    half = pair_add(kept, exchange(sent, flips(size, 1)))
    for step in (2, 8, 32):
        first = exchange(half, flips(size, step))
        second = exchange(half, flips(size, 2 * step))
        third = exchange(half, flips(size, 3 * step))
        half = pair_add(pair_add(half, first), pair_add(second, third))
    half = pair_add(half, exchange(half, flips(size, 224)))
    return half, exchange(half, flips(size, 1))


def power_scale(square):
    scale = jnp.ones_like(square)
    inverse = jnp.ones_like(square)
    for k in (32, 16, 8, 4, 2, 1):
        big = square >= 4.0**k
        square = jnp.where(big, square * 4.0**-k, square)
        scale = jnp.where(big, scale * 2.0**-k, scale)
        inverse = jnp.where(big, inverse * 2.0**k, inverse)
    for k in (32, 16, 8, 4, 2, 1):
        small = square < 4.0 ** (1 - k)
        square = jnp.where(small, square * 4.0**k, square)
        scale = jnp.where(small, scale * 2.0**k, scale)
        inverse = jnp.where(small, inverse * 2.0**-k, inverse)
    return scale, inverse


def slices(high, low, unit, count):
    out = []
    rest = high
    for index in range(count):
        if index == 2 and low is not None:
            rest = rest + low
        magic = 1.5 * 2.0**23 * unit * 2.0 ** (-9 * index)
        piece = (rest + magic) - magic
        rest = rest - piece
        out.append(piece)
    return out


def add_levels(levels):
    total, rest = two_sum(levels[0], levels[1])
    for level in levels[2:4]:
        total, error = two_sum(total, level)
        rest = rest + error
    for level in levels[4:]:
        rest = rest + level
    return two_sum(total, rest)


def factor(matrix, size=32):
    count = 128 // size
    work = [matrix[size * i : size * i + size] for i in range(count)]
    lanes, rows = iota((size, 128), 1), iota((size, 128), 0)
    tile_rows = iota((8, 128), 0)
    extra = [jnp.where(lanes == rows + size * i, 1.0, 0.0).astype(F32) for i in range(count)]
    tiles = size // 8

    def spread(row):
        return jnp.broadcast_to(row, (8, 128))

    upper, inverse = [], []
    for block in range(count):
        at = size * block
        wide = [work[block][8 * t : 8 * t + 8] for t in range(tiles)]
        carried = [extra[block][8 * t : 8 * t + 8] for t in range(tiles)]
        columns = [
            [None if t < k // 8 else spread(wide[t][:, at + k : at + k + 1]) for t in range(tiles)] for k in range(size)
        ]
        pivots = [jnp.ones((8, 128), F32) for _ in range(tiles)]
        for j in range(size):
            own, row = j // 8, j % 8
            pivot = columns[j][own][row : row + 1]
            pivots[own] = jnp.where(tile_rows == row, spread(pivot), pivots[own])
            if j == size - 1:
                break
            factor_row = spread(1.0 / pivot)
            wide_row, carried_row = spread(wide[own][row : row + 1]), spread(carried[own][row : row + 1])
            ratio = [None] * tiles
            for t in range(own, tiles):
                ratio[t] = columns[j][t] * factor_row
                if t == own:
                    ratio[t] = jnp.where(tile_rows > row, ratio[t], 0.0)
            for k in range(j + 1, size):
                entry = spread(columns[j][k // 8][k % 8 : k % 8 + 1])
                for t in range(k // 8, tiles):
                    columns[k][t] = columns[k][t] - ratio[t] * entry
            for t in range(own, tiles):
                wide[t] = wide[t] - ratio[t] * wide_row
                carried[t] = carried[t] - ratio[t] * carried_row
        pivots = jnp.concatenate(pivots, axis=0)
        root = lax.rsqrt(pivots)
        root = root * (1.5 - 0.5 * pivots * root * root)
        wide = jnp.where(lanes >= rows + at, jnp.concatenate(wide, axis=0) * root, 0.0)
        carried = jnp.concatenate(carried, axis=0) * root
        upper.append(wide)
        inverse.append(carried)
        if block < count - 1:
            left = split3(wide)
            right = split3(jnp.concatenate([wide, carried], axis=1))
            order = ((0, 0), (0, 1), (1, 0), (1, 1), (0, 2), (2, 0))
            update = dot(
                jnp.concatenate([left[i] for i, _ in order], axis=0),
                jnp.concatenate([right[j] for _, j in order], axis=0),
                TN,
            )
            for later in range(block + 1, count):
                at = size * later
                work[later] = work[later] - update[at : at + size, :128]
                extra[later] = extra[later] - update[at : at + size, 128:]
    return jnp.concatenate(upper, axis=0), jnp.concatenate(inverse, axis=0)


def finish_body(
    root,
    out_chunk,
    mine_ref,
    other_ref,
    table_ref,
    index_ref,
    coef_ref,
    x_ref,
    modes_ref,
    operator_ref,
    factor_ref,
    y_ref,
    shift_ref,
    small_ref,
    small_sems,
    out_sems,
):
    columns = x_ref.shape[1]
    own = iota((16, 16), 0) == iota((16, 16), 1)
    index = jnp.sum(jnp.where(own, index_ref[...], 0), axis=1, keepdims=True)
    coef = jnp.sum(jnp.where(own, coef_ref[...], 0.0), axis=1, keepdims=True)
    onehot = (iota((16, 128), 1) == index).astype(F32)
    chosen = dot(onehot, table_ref[...], NT, HIGH) * (coef * root)
    even = even_core()
    mine, other = mine_ref[...], other_ref[...]
    packed = jnp.concatenate([jnp.where(even, mine, other), jnp.where(even, other, mine)], axis=1)
    gram_high, last_high = unpack(packed[0])
    gram_low, last_low = unpack(packed[1])
    gram_high, gram_low = two_sum(gram_high, gram_low)
    last_high, last_low = two_sum(last_high, last_low)
    on_diagonal = iota((128, 128), 0) == iota((128, 128), 1)
    diagonal = jnp.sum(jnp.where(on_diagonal, gram_high, 0.0), axis=0, keepdims=True)
    scale, unscale = power_scale(diagonal)
    scale_wide = jnp.broadcast_to(scale, (128, 128))
    scale_tall = scale_wide.T
    gram_high = gram_high * scale_wide * scale_tall
    gram_low = gram_low * scale_wide * scale_tall
    last_high = last_high * scale
    last_low = last_low * scale
    biggest = jnp.max(jnp.abs(last_high), axis=1, keepdims=True)
    last_scale, last_unscale = power_scale(jnp.broadcast_to(biggest * biggest, (1, 128)))
    last_high = last_high * last_scale
    last_low = last_low * last_scale

    upper, lower_inverse = factor(gram_high)
    small_ref[0] = upper * (unscale * (1.0 / root))
    factor_out = pltpu.make_async_copy(small_ref.at[0], factor_ref, small_sems.at[0])
    factor_out.start()

    norms = jnp.sum(lower_inverse * lower_inverse, axis=1, keepdims=True)
    row_scale, _ = power_scale(jnp.broadcast_to(norms, (128, 128)))
    y_one, y_two = slices(lower_inverse * row_scale, None, 2.0**-7, 2)
    first = y_one + y_two
    y_both = jnp.concatenate([y_one, y_two], axis=0).astype(BF16)

    blank = jnp.zeros((7, 128), F32)
    whole_high = jnp.concatenate([gram_high, last_high, blank], axis=0)
    whole_low = jnp.concatenate([gram_low, last_low, blank], axis=0)
    g = [piece.astype(BF16) for piece in slices(whole_high, whole_low, 2.0**-6, 4)]
    p = [dot(piece, y_both, NT) for piece in g]
    one = [piece[:, :128] for piece in p]
    two = [piece[:, 128:] for piece in p]
    t_high, t_low = add_levels(
        [one[0], one[1] + two[0], one[2] + two[1], one[3] + two[2], two[3]]
    )

    norms = jnp.sum(t_high[:128] * t_high[:128], axis=0, keepdims=True)
    column_scale, column_unscale = power_scale(norms)
    t = slices(t_high[:128] * column_scale, t_low[:128] * column_scale, 2.0**-7, 4)
    t_all = jnp.concatenate([piece.astype(BF16) for piece in t], axis=1)
    s = dot(y_both, t_all, NN)
    one = [s[:128, 128 * k : 128 * k + 128] for k in range(4)]
    two = [s[128:, 128 * k : 128 * k + 128] for k in range(4)]
    s_high, s_low = add_levels(
        [one[0], one[1] + two[0], one[2] + two[1], one[3] + two[2], two[3]]
    )
    _, second = factor((s_high + s_low) * column_unscale)

    whole = dot(second, first, NN, HIGH)
    shift_ref[...] = t_high
    z = shift_ref[1:129]
    following = jnp.where(iota((1, 128), 1) == 127, last_unscale, pltpu.roll(unscale, 127, 1))
    h = dot(whole * (scale * following), z, NN, HIGH)
    small_ref[1] = dot(second, h, NT, HIGH)
    operator_out = pltpu.make_async_copy(small_ref.at[1], operator_ref, small_sems.at[1])
    operator_out.start()
    comb = dot(chosen, whole, NN, HIGH) * scale

    shifted = jnp.where(iota(comb.shape, 1) == 0, 0.0, pltpu.roll(comb, 1, 1))
    c = split3(shifted)
    left = jnp.concatenate(
        [
            jnp.concatenate([c[0], c[1]], axis=1),
            jnp.concatenate([c[1], c[0]], axis=1),
            jnp.concatenate([c[2], jnp.zeros_like(c[2])], axis=1),
        ],
        axis=0,
    )

    def send(index):
        at = pl.ds(pl.multiple_of(index * out_chunk, out_chunk), out_chunk)
        return pltpu.make_async_copy(y_ref.at[:, at], modes_ref.at[:, at], out_sems.at[index])

    def step(index, carry):
        at = pl.ds(pl.multiple_of(index * out_chunk, out_chunk), out_chunk)
        x_high, x_mid, x_low = split3(x_ref[0:128, at])
        main = dot(left, jnp.concatenate([x_high, x_mid], axis=0), NN)
        side = dot(c[0], x_low, NN)
        end = comb[:, 127:128] * x_ref[128:129, at]
        y_ref[:, at] = (main[0:16] + end) + (main[16:32] + (main[32:48] + side))
        send(index).start()
        return carry

    lax.fori_loop(0, columns // out_chunk, step, 0)
    for index in range(columns // out_chunk):
        send(index).wait()
    factor_out.wait()
    operator_out.wait()


def finish(mine, other, table, index, coef, panel, root, out_chunk=4096):
    modes, columns = index.shape[0], panel.shape[1]
    whole = pl.BlockSpec(memory_space=pltpu.VMEM)
    remote = pl.BlockSpec(memory_space=pl.ANY)
    return pl.pallas_call(
        functools.partial(finish_body, root, out_chunk),
        in_specs=[whole] * 6,
        out_specs=[remote] * 3,
        out_shape=[
            jax.ShapeDtypeStruct((modes, columns), F32),
            jax.ShapeDtypeStruct((128, 128), F32),
            jax.ShapeDtypeStruct((128, 128), F32),
        ],
        scratch_shapes=[
            pltpu.VMEM((modes, columns), F32),
            pltpu.VMEM((136, 128), F32),
            pltpu.VMEM((2, 128, 128), F32),
            pltpu.SemaphoreType.DMA((2,)),
            pltpu.SemaphoreType.DMA((columns // out_chunk,)),
        ],
        compiler_params=pltpu.CompilerParams(vmem_limit_bytes=LIMIT),
        name="finish",
    )(mine, other, table, index.reshape(1, modes), coef.reshape(1, modes), panel)


def local(size, panel, eig_table, mode_index, mode_coef):
    root = float(panel.shape[1] * size) ** 0.5
    kept, sent, held = local_gram(panel)
    mine, other = sum_pairs(kept, sent, size)
    return tuple(finish(mine, other, eig_table, mode_index, mode_coef, held, root))


def solution(mesh):
    return jax.shard_map(
        functools.partial(local, mesh.shape["space"]),
        mesh=mesh,
        in_specs=(P(None, "space"), P(), P(), P()),
        out_specs=(P(None, "space"), P(), P()),
        check_vma=False,
    )
```

```python
import functools

import jax
import jax.numpy as jnp
from jax import lax
from jax.experimental import pallas as pl
from jax.experimental.pallas import tpu as pltpu
from jax.sharding import PartitionSpec as P

HIGH = lax.Precision.HIGHEST
F32 = jnp.float32
BF16 = jnp.bfloat16
NT = (((1,), (1,)), ((), ()))
NN = (((1,), (0,)), ((), ()))
TN = (((0,), (0,)), ((), ()))
HALF = 40
GRAM_LIMIT = 50 * 1024 * 1024
LIMIT = 32 * 1024 * 1024


def dot(a, b, dims, precision=None):
    return lax.dot_general(a, b, dims, precision=precision, preferred_element_type=F32)


def dot_six(a, b, turn=False):
    left, right = split3(a), split3(b)
    order = ((0, 0), (0, 1), (1, 0), (1, 1), (0, 2), (2, 0))
    stack = jnp.concatenate([left[i] for i, _ in order], axis=1)
    if turn:
        return dot(stack, jnp.concatenate([right[j] for _, j in order], axis=1), NT)
    return dot(stack, jnp.concatenate([right[j] for _, j in order], axis=0), NN)


def two_sum(a, b):
    total = a + b
    other = total - a
    return total, (a - (total - other)) + (b - other)


def split3(x):
    high = x.astype(BF16)
    rest = x - high.astype(F32)
    mid = rest.astype(BF16)
    return high, mid, (rest - mid.astype(F32)).astype(BF16)


def iota(shape, axis):
    return lax.broadcasted_iota(jnp.int32, shape, axis)


def gram_body(
    chunk,
    part,
    panel_ref,
    kept_ref,
    sent_ref,
    x_ref,
    high_ref,
    low_ref,
    cross_ref,
    mid_ref,
    last_ref,
    sems,
):
    count = panel_ref.shape[1] // chunk
    for index in range(count):
        fetch(panel_ref, x_ref, sems, chunk, index).start()
    for ref in (high_ref, low_ref, cross_ref, mid_ref, last_ref):
        ref[...] = jnp.zeros_like(ref)

    def step(index, carry):
        fetch(panel_ref, x_ref, sems, chunk, index).wait()
        for start in range(0, chunk, part):
            at = pl.ds(pl.multiple_of(index * chunk + start, part), part)
            x = x_ref[0:128, at]
            high, mid, low = split3(x)
            main = dot(jnp.concatenate([high, low], axis=0), jnp.concatenate([high, mid], axis=0), NT)
            total, rest = two_sum(high_ref[...], main[:128, :128])
            high_ref[...] = total
            low_ref[...] += rest
            cross_ref[...] += main[:128, 128:] + (main[128:, :128] + main[128:, 128:])
            mid_ref[...] += dot(mid, mid, NT)
            end = x_ref[128:129, at]
            partial = x[:, 0:128] * end[:, 0:128]
            for tile in range(128, part, 128):
                partial = partial + x[:, tile : tile + 128] * end[:, tile : tile + 128]
            last_ref[...] += partial
        return carry

    lax.fori_loop(0, count, step, 0)
    cross = cross_ref[...]
    rest = low_ref[...] + (mid_ref[...] + (cross + cross.T))
    high, low = two_sum(high_ref[...], rest)
    turned = last_ref[...].T
    end_high = turned[0:8]
    end_low = jnp.zeros_like(end_high)
    for row in range(8, 128, 8):
        end_high, error = two_sum(end_high, turned[row : row + 8])
        end_low = end_low + error
    row_high, row_low = end_high[0:1], end_low[0:1]
    for row in range(1, 8):
        row_high, error = two_sum(row_high, end_high[row : row + 1])
        row_low = row_low + (error + end_low[row : row + 1])
    even = even_core()
    for place, (gram, last) in enumerate(((high, row_high), (low, row_low))):
        packed = pack(gram, last)
        kept_ref[place] = jnp.where(even, packed[:HALF], packed[HALF:])
        sent_ref[place] = jnp.where(even, packed[HALF:], packed[:HALF])


def even_core():
    return lax.axis_index("space") % 2 == 0


def fetch(panel_ref, x_ref, sems, chunk, index):
    at = pl.ds(pl.multiple_of(index * chunk, chunk), chunk)
    return pltpu.make_async_copy(panel_ref.at[:, at], x_ref.at[:, at], sems.at[index])


def pack(gram, last):
    rows, lanes = iota((64, 128), 0), iota((64, 128), 1)
    turned = pltpu.roll(gram[64:128], 64, 1)
    folded = jnp.where(lanes > rows, gram[0:64], jnp.where(lanes < rows, turned, 0.0))
    on_diagonal = iota((128, 128), 0) == iota((128, 128), 1)
    diagonal = jnp.sum(jnp.where(on_diagonal, gram, 0.0), axis=0, keepdims=True)
    return jnp.concatenate([folded, diagonal, last, jnp.zeros((2 * HALF - 66, 128), F32)], axis=0)


def unpack(packed):
    rows, lanes = iota((64, 128), 0), iota((64, 128), 1)
    folded = packed[0:64]
    top = jnp.where(lanes > rows, folded, 0.0)
    turned = pltpu.roll(folded, 64, 1)
    bottom = jnp.where((lanes >= 64) & (lanes - 64 < rows), turned, 0.0)
    half = jnp.concatenate([top, bottom], axis=0)
    on_diagonal = iota((128, 128), 0) == iota((128, 128), 1)
    gram = jnp.where(on_diagonal, packed[64:65], half + half.T)
    return gram, packed[65:66]


def local_gram(panel, chunk=4096, part=1024):
    snaps, columns = panel.shape
    square = pltpu.VMEM((128, 128), F32)
    return pl.pallas_call(
        functools.partial(gram_body, chunk, part),
        in_specs=[pl.BlockSpec(memory_space=pl.ANY)],
        out_shape=[pltpu.VMEM((2, HALF, 128), F32)] * 2
        + [pltpu.VMEM((snaps, columns), F32)],
        out_specs=[pl.BlockSpec(memory_space=pltpu.VMEM)] * 3,
        scratch_shapes=[square] * 5
        + [pltpu.SemaphoreType.DMA((columns // chunk,))],
        compiler_params=pltpu.CompilerParams(vmem_limit_bytes=GRAM_LIMIT),
        name="gram",
    )(panel)


def pair_add(a, b):
    total, rest = two_sum(a[0], b[0])
    return jnp.stack([total, (a[1] + b[1]) + rest])


def exchange(x, pairs):
    return lax.ppermute(x, "space", pairs)


def flips(size, step):
    return [(i, i ^ step) for i in range(size)]


def sum_pairs(kept, sent, size):
    half = pair_add(kept, exchange(sent, flips(size, 1)))
    for step in (2, 8, 32):
        first = exchange(half, flips(size, step))
        second = exchange(half, flips(size, 2 * step))
        third = exchange(half, flips(size, 3 * step))
        half = pair_add(pair_add(half, first), pair_add(second, third))
    half = pair_add(half, exchange(half, flips(size, 224)))
    return half, exchange(half, flips(size, 1))


def power_scale(square):
    scale = jnp.ones_like(square)
    inverse = jnp.ones_like(square)
    for k in (32, 16, 8, 4, 2, 1):
        big = square >= 4.0**k
        square = jnp.where(big, square * 4.0**-k, square)
        scale = jnp.where(big, scale * 2.0**-k, scale)
        inverse = jnp.where(big, inverse * 2.0**k, inverse)
    for k in (32, 16, 8, 4, 2, 1):
        small = square < 4.0 ** (1 - k)
        square = jnp.where(small, square * 4.0**k, square)
        scale = jnp.where(small, scale * 2.0**k, scale)
        inverse = jnp.where(small, inverse * 2.0**-k, inverse)
    return scale, inverse


def slices(high, low, unit, count):
    out = []
    rest = high
    for index in range(count):
        if index == 2 and low is not None:
            rest = rest + low
        magic = 1.5 * 2.0**23 * unit * 2.0 ** (-9 * index)
        piece = (rest + magic) - magic
        rest = rest - piece
        out.append(piece)
    return out


def add_levels(levels):
    total, rest = two_sum(levels[0], levels[1])
    for level in levels[2:4]:
        total, error = two_sum(total, level)
        rest = rest + error
    for level in levels[4:]:
        rest = rest + level
    return two_sum(total, rest)


def factor(matrix, size=32):
    count = 128 // size
    work = [matrix[size * i : size * i + size] for i in range(count)]
    lanes, rows = iota((size, 128), 1), iota((size, 128), 0)
    tile_rows = iota((8, 128), 0)
    extra = [jnp.where(lanes == rows + size * i, 1.0, 0.0).astype(F32) for i in range(count)]
    tiles = size // 8

    def spread(row):
        return jnp.broadcast_to(row, (8, 128))

    upper, inverse = [], []
    for block in range(count):
        at = size * block
        wide = [work[block][8 * t : 8 * t + 8] for t in range(tiles)]
        carried = [extra[block][8 * t : 8 * t + 8] for t in range(tiles)]
        columns = [
            [None if t < k // 8 else spread(wide[t][:, at + k : at + k + 1]) for t in range(tiles)] for k in range(size)
        ]
        pivots = [jnp.ones((8, 128), F32) for _ in range(tiles)]
        for j in range(size):
            own, row = j // 8, j % 8
            pivot = columns[j][own][row : row + 1]
            pivots[own] = jnp.where(tile_rows == row, spread(pivot), pivots[own])
            if j == size - 1:
                break
            factor_row = spread(1.0 / pivot)
            wide_row, carried_row = spread(wide[own][row : row + 1]), spread(carried[own][row : row + 1])
            ratio = [None] * tiles
            for t in range(own, tiles):
                ratio[t] = columns[j][t] * factor_row
                if t == own:
                    ratio[t] = jnp.where(tile_rows > row, ratio[t], 0.0)
            for k in range(j + 1, size):
                entry = spread(columns[j][k // 8][k % 8 : k % 8 + 1])
                for t in range(k // 8, tiles):
                    columns[k][t] = columns[k][t] - ratio[t] * entry
            for t in range(own, tiles):
                wide[t] = wide[t] - ratio[t] * wide_row
                carried[t] = carried[t] - ratio[t] * carried_row
        pivots = jnp.concatenate(pivots, axis=0)
        root = lax.rsqrt(pivots)
        root = root * (1.5 - 0.5 * pivots * root * root)
        wide = jnp.where(lanes >= rows + at, jnp.concatenate(wide, axis=0) * root, 0.0)
        carried = jnp.concatenate(carried, axis=0) * root
        upper.append(wide)
        inverse.append(carried)
        if block < count - 1:
            left = split3(wide)
            right = split3(jnp.concatenate([wide, carried], axis=1))
            order = ((0, 0), (0, 1), (1, 0), (1, 1), (0, 2), (2, 0))
            update = dot(
                jnp.concatenate([left[i] for i, _ in order], axis=0),
                jnp.concatenate([right[j] for _, j in order], axis=0),
                TN,
            )
            for later in range(block + 1, count):
                at = size * later
                work[later] = work[later] - update[at : at + size, :128]
                extra[later] = extra[later] - update[at : at + size, 128:]
    return jnp.concatenate(upper, axis=0), jnp.concatenate(inverse, axis=0)


def finish_body(
    root,
    out_chunk,
    mine_ref,
    other_ref,
    table_ref,
    index_ref,
    coef_ref,
    x_ref,
    modes_ref,
    operator_ref,
    factor_ref,
    y_ref,
    shift_ref,
    small_ref,
    small_sems,
    out_sems,
):
    columns = x_ref.shape[1]
    own = iota((16, 16), 0) == iota((16, 16), 1)
    index = jnp.sum(jnp.where(own, index_ref[...], 0), axis=1, keepdims=True)
    coef = jnp.sum(jnp.where(own, coef_ref[...], 0.0), axis=1, keepdims=True)
    onehot = (iota((16, 128), 1) == index).astype(F32)
    chosen = dot(onehot, table_ref[...], NT, HIGH) * (coef * root)
    even = even_core()
    mine, other = mine_ref[...], other_ref[...]
    packed = jnp.concatenate([jnp.where(even, mine, other), jnp.where(even, other, mine)], axis=1)
    gram_high, last_high = unpack(packed[0])
    gram_low, last_low = unpack(packed[1])
    gram_high, gram_low = two_sum(gram_high, gram_low)
    last_high, last_low = two_sum(last_high, last_low)
    on_diagonal = iota((128, 128), 0) == iota((128, 128), 1)
    diagonal = jnp.sum(jnp.where(on_diagonal, gram_high, 0.0), axis=0, keepdims=True)
    scale, unscale = power_scale(diagonal)
    scale_wide = jnp.broadcast_to(scale, (128, 128))
    scale_tall = scale_wide.T
    gram_high = gram_high * scale_wide * scale_tall
    gram_low = gram_low * scale_wide * scale_tall
    last_high = last_high * scale
    last_low = last_low * scale
    biggest = jnp.max(jnp.abs(last_high), axis=1, keepdims=True)
    last_scale, last_unscale = power_scale(jnp.broadcast_to(biggest * biggest, (1, 128)))
    last_high = last_high * last_scale
    last_low = last_low * last_scale

    upper, lower_inverse = factor(gram_high)
    small_ref[0] = upper * (unscale * (1.0 / root))
    factor_out = pltpu.make_async_copy(small_ref.at[0], factor_ref, small_sems.at[0])
    factor_out.start()

    norms = jnp.sum(lower_inverse * lower_inverse, axis=1, keepdims=True)
    row_scale, _ = power_scale(jnp.broadcast_to(norms, (128, 128)))
    y_one, y_two = slices(lower_inverse * row_scale, None, 2.0**-7, 2)
    first = y_one + y_two
    y_both = jnp.concatenate([y_one, y_two], axis=0).astype(BF16)

    blank = jnp.zeros((7, 128), F32)
    whole_high = jnp.concatenate([gram_high, last_high, blank], axis=0)
    whole_low = jnp.concatenate([gram_low, last_low, blank], axis=0)
    g = [piece.astype(BF16) for piece in slices(whole_high, whole_low, 2.0**-6, 4)]
    p = [dot(piece, y_both, NT) for piece in g]
    one = [piece[:, :128] for piece in p]
    two = [piece[:, 128:] for piece in p]
    t_high, t_low = add_levels(
        [one[0], one[1] + two[0], one[2] + two[1], one[3] + two[2], two[3]]
    )

    norms = jnp.sum(t_high[:128] * t_high[:128], axis=0, keepdims=True)
    column_scale, column_unscale = power_scale(norms)
    t = slices(t_high[:128] * column_scale, t_low[:128] * column_scale, 2.0**-7, 4)
    t_all = jnp.concatenate([piece.astype(BF16) for piece in t], axis=1)
    s = dot(y_both, t_all, NN)
    one = [s[:128, 128 * k : 128 * k + 128] for k in range(4)]
    two = [s[128:, 128 * k : 128 * k + 128] for k in range(4)]
    s_high, s_low = add_levels(
        [one[0], one[1] + two[0], one[2] + two[1], one[3] + two[2], two[3]]
    )
    _, second = factor((s_high + s_low) * column_unscale)

    whole = dot_six(second, first)
    shift_ref[...] = t_high
    z = shift_ref[1:129]
    following = jnp.where(iota((1, 128), 1) == 127, last_unscale, pltpu.roll(unscale, 127, 1))
    h = dot_six(whole * (scale * following), z)
    small_ref[1] = dot_six(second, h, True)
    operator_out = pltpu.make_async_copy(small_ref.at[1], operator_ref, small_sems.at[1])
    operator_out.start()
    comb = dot_six(chosen, whole) * scale

    shifted = jnp.where(iota(comb.shape, 1) == 0, 0.0, pltpu.roll(comb, 1, 1))
    c = split3(shifted)
    left = jnp.concatenate(
        [
            jnp.concatenate([c[0], c[1]], axis=1),
            jnp.concatenate([c[1], c[0]], axis=1),
            jnp.concatenate([c[2], jnp.zeros_like(c[2])], axis=1),
        ],
        axis=0,
    )

    def send(index):
        at = pl.ds(pl.multiple_of(index * out_chunk, out_chunk), out_chunk)
        return pltpu.make_async_copy(y_ref.at[:, at], modes_ref.at[:, at], out_sems.at[index])

    def step(index, carry):
        at = pl.ds(pl.multiple_of(index * out_chunk, out_chunk), out_chunk)
        x_high, x_mid, x_low = split3(x_ref[0:128, at])
        main = dot(left, jnp.concatenate([x_high, x_mid], axis=0), NN)
        side = dot(c[0], x_low, NN)
        end = comb[:, 127:128] * x_ref[128:129, at]
        y_ref[:, at] = (main[0:16] + end) + (main[16:32] + (main[32:48] + side))
        send(index).start()
        return carry

    lax.fori_loop(0, columns // out_chunk, step, 0)
    for index in range(columns // out_chunk):
        send(index).wait()
    factor_out.wait()
    operator_out.wait()


def finish(mine, other, table, index, coef, panel, root, out_chunk=4096):
    modes, columns = index.shape[0], panel.shape[1]
    whole = pl.BlockSpec(memory_space=pltpu.VMEM)
    remote = pl.BlockSpec(memory_space=pl.ANY)
    return pl.pallas_call(
        functools.partial(finish_body, root, out_chunk),
        in_specs=[whole] * 6,
        out_specs=[remote] * 3,
        out_shape=[
            jax.ShapeDtypeStruct((modes, columns), F32),
            jax.ShapeDtypeStruct((128, 128), F32),
            jax.ShapeDtypeStruct((128, 128), F32),
        ],
        scratch_shapes=[
            pltpu.VMEM((modes, columns), F32),
            pltpu.VMEM((136, 128), F32),
            pltpu.VMEM((2, 128, 128), F32),
            pltpu.SemaphoreType.DMA((2,)),
            pltpu.SemaphoreType.DMA((columns // out_chunk,)),
        ],
        compiler_params=pltpu.CompilerParams(vmem_limit_bytes=LIMIT),
        name="finish",
    )(mine, other, table, index.reshape(1, modes), coef.reshape(1, modes), panel)


def local(size, panel, eig_table, mode_index, mode_coef):
    root = float(panel.shape[1] * size) ** 0.5
    kept, sent, held = local_gram(panel)
    mine, other = sum_pairs(kept, sent, size)
    return tuple(finish(mine, other, eig_table, mode_index, mode_coef, held, root))


def solution(mesh):
    return jax.shard_map(
        functools.partial(local, mesh.shape["space"]),
        mesh=mesh,
        in_specs=(P(None, "space"), P(), P(), P()),
        out_specs=(P(None, "space"), P(), P()),
        check_vma=False,
    )
```
